32 devices in a mesh: tile: 8 (over y, x, core), rad: 4 (over z).
Axes of the slice: x: 2, y: 2, z: 4, core: 2. Of those that a mesh axis runs over, the one named last changes fastest.
Arguments:
- fields: float32 [3072, 1, 512], P('tile', None, 'rad'), may hold values from -6 to 6
- velocity: float32 [3072, 2, 512], P('tile', None, 'rad'), may hold values from -6 to 6
- operators: bfloat16 [24, 3, 128, 896], P('tile'), may hold values from -0.1875 to 0.1875
- neighbours: int32 [24, 7], P('tile'), may hold values from 0 to 23, as said below
- kappa_ref: float32 [512], replicated, may hold values from 0.3 to 3
- quad_weight: float32 [3072], P('tile'), may hold values from 0.5 to 2
- basis: float32 [3072, 512], P('tile'), may hold values from -0.375 to 0.375
- degree: int32 [512], replicated, may hold values from 0 to 22
Outputs:
- filtered: float32 [3072, 1, 512], P('tile', None, 'rad')
The draws below stay inside these ranges and needn't reach their ends.
Inputs may be any that keep to these rules, and one draw needn't show every extreme that they name: `neighbours`: row b lists seven different blocks; the first is b itself, and each lies in the tile of b (block // 3) or in one of the two tiles beside it, counted cyclically over the 8 tiles; every row names at least one block of each of the two tiles beside its own.
All inputs are finite; a program needn't handle non-finite values.
Results may differ from the reference program's by a relative error of at most 0.0011.
Values may be sent and summed in bfloat16 or wider, within the bound.
No kernel may reach another device: no remote copies, remote signals or barrier semaphores. Data moves between devices by JAX's collectives and lax.ppermute only.
A program may use at most 64 MiB of HBM per device.

```python
import math
import jax
import jax.numpy as jnp
from jax import lax

FIELDS = 1
NR = 512
MODES = 512
DEGMAX = 22
BS = 128
BLK_DEV = 3
NBLK = 24
NODES = 3072


def draw_neighbours(key, part):
    candidates = 3 * BLK_DEV
    key_left, key_right, key_rest = jax.random.split(key, 3)
    blocks = jnp.arange(NBLK, dtype=jnp.int32)
    home = BLK_DEV + blocks % BLK_DEV
    left_pick = jax.random.randint(key_left, (NBLK,), 0, BLK_DEV, dtype=jnp.int32)
    right_pick = jax.random.randint(key_right, (NBLK,), 2 * BLK_DEV, 3 * BLK_DEV, dtype=jnp.int32)
    slots = jnp.arange(candidates, dtype=jnp.int32)[None, :]
    scores = jax.random.randint(key_rest, (NBLK, candidates), 0, 1 << 20, dtype=jnp.int32) * candidates + slots
    scores = jnp.where(slots == home[:, None], -3, scores)
    scores = jnp.where(slots == left_pick[:, None], -2, scores)
    scores = jnp.where(slots == right_pick[:, None], -1, scores)
    chosen = jnp.argsort(scores, axis=1, stable=True)[:, :7].astype(jnp.int32)
    tile_of = blocks // BLK_DEV
    return ((tile_of[:, None] - 1) * BLK_DEV + chosen + NBLK) % NBLK


def plant(array, key, least, largest):
    index_at = [jax.random.randint(jax.random.fold_in(key, axis), (), 0, length) for axis, length in enumerate(array.shape)]
    widest = array.shape.index(max(array.shape))
    next_to = index_at[:widest] + [(index_at[widest] + 1) % array.shape[widest]] + index_at[widest + 1:]
    return array.at[tuple(index_at)].set(least).at[tuple(next_to)].set(largest)


def spiked(result, rng, source, target, parts, factor):
    def block_of(position):
        return (jnp.arange(result.shape[position]) // (result.shape[position] // parts)).reshape((-1,) + (1,) * (result.ndim - 1 - position))

    one_side = jax.random.permutation(rng, parts)[block_of(target)]
    other_side = (block_of(target) + parts // 2) % parts
    return jnp.where((block_of(source) == one_side) | (block_of(source) == other_side), factor * result, result)


def level_of(stream_key, dims, cuts, least, top_value):
    level, own = 1.0, jax.random.fold_in(stream_key, 6)
    for dim, shards_of in cuts:
        steps = jnp.exp(jax.random.uniform(jax.random.fold_in(own, dim), (shards_of,), jnp.float32, least / len(cuts), top_value / len(cuts)))
        level = level * jnp.repeat(steps, dims[dim] // shards_of).reshape([-1 if axis == dim else 1 for axis in range(len(dims))])
    return level


def scatter_about(key, dims, width, bound, cuts=(), held_as=jnp.bfloat16):
    factor_of = level_of(key, dims, cuts, -0.22, 0.18) if cuts else 1.0
    result = jax.random.normal(key, dims, jnp.float32) * width * factor_of
    return jnp.minimum(jnp.maximum(result, -bound), bound).astype(held_as)


def bell_draw_with(rng, extent, deviation, most, cuts, heavy, kind=jnp.bfloat16):
    values = deviation * jax.random.normal(rng, extent, jnp.float32)
    if cuts:
        values = values * level_of(rng, extent, cuts, -0.22, 0.18)
    return jnp.clip(spiked(values, jax.random.fold_in(rng, 3), *heavy), -most, most).astype(kind)


def setup_inputs(seed: int = 0) -> dict:
    key_of = jax.random.split(jax.random.key(seed), 9)
    return {
        "fields": scatter_about(key_of[0], (NODES, FIELDS, NR), 1.0, 6.0, ((0, 8), (2, 4)), jnp.float32),
        "velocity": scatter_about(key_of[1], (NODES, 2, NR), 1.0, 6.0, ((0, 8), (2, 4)), jnp.float32),
        "operators": scatter_about(key_of[2], (NBLK, 3, BS, 7 * BS), (7 * BS) ** -0.5, 0.1875, ((0, 8),)),
        "neighbours": draw_neighbours(jax.random.fold_in(key_of[8], 71), 0),
        "kappa_ref": jnp.clip(jnp.exp(jax.random.uniform(key_of[4], (NR,), jnp.float32, math.log(0.3), math.log(3.0))), 0.3, 3.0),
        "quad_weight": jnp.clip(jnp.exp(math.log(2.0) - 1.3862944 * jax.random.uniform(key_of[5], (NODES,), jnp.float32) ** level_of(key_of[5], (NODES,), ((0, 8),), -0.2, 0.2)), 0.5, 2.0),
        "basis": bell_draw_with(key_of[6], (NODES, MODES), MODES ** -0.5, 0.375, ((0, 8),), (0, 1, 8, 2.0), jnp.float32),
        "degree": plant(jax.random.randint(key_of[7], (MODES,), 0, DEGMAX + 1), jax.random.fold_in(key_of[7], 1), 0, DEGMAX).astype(jnp.int32),
    }


advect_step = 0.25
hyper_rate = 0.1
radial_step = 0.25

def cheb_matrix(count):
    points = jnp.arange(count, dtype=jnp.int32)
    angles = jnp.pi * points.astype(jnp.float32) / (count - 1)
    upper = angles[:, None]
    lower = angles[None, :]
    spacing = -2.0 * jnp.sin((upper + lower) / 2.0) * jnp.sin((upper - lower) / 2.0)
    on_diag = points[:, None] == points[None, :]
    spacing = jnp.where(on_diag, jnp.float32(1.0), spacing)
    weights = jnp.where((points == 0) | (points == count - 1), jnp.float32(2.0), jnp.float32(1.0))
    parity = jnp.where((points[:, None] + points[None, :]) % 2 == 0, jnp.float32(1.0), jnp.float32(-1.0))
    entries = weights[:, None] / weights[None, :] * parity / spacing
    entries = jnp.where(on_diag, jnp.float32(0.0), entries)
    diagonal = -lax.optimization_barrier(jnp.sum(entries, axis=1))
    matrix = entries + jnp.diag(diagonal)
    return jnp.sin(angles)[:, None] * matrix / count

def reference(fields, velocity, operators, neighbours, kappa_ref, quad_weight, basis, degree):
    nodes, nfield, levels = fields.shape
    nblock, _, block_size, _ = operators.shape
    columns = nfield * levels
    cell_rows = fields.astype(jnp.bfloat16).reshape(nblock, block_size, columns)
    vel_blocks = velocity.reshape(nblock, block_size, 2, 1, levels)

    def first_block(packed):
        block_ops, nearby_ids, vel_block = packed
        nearby = jnp.take(cell_rows, nearby_ids, axis=0).reshape(7 * block_size, columns)
        products = jnp.einsum('kij,jc->kic', block_ops.astype(jnp.float32), nearby.astype(jnp.float32), precision=lax.Precision.HIGHEST)
        products = products.reshape(3, block_size, nfield, levels)
        advect = vel_block[:, 0] * products[0] + vel_block[:, 1] * products[1]
        return (advect, products[2])
    advect, lap_one = lax.map(first_block, (operators, neighbours, vel_blocks))
    lap_round = lap_one.astype(jnp.bfloat16).reshape(nblock, block_size, columns)

    def second_block(packed):
        block_ops, nearby_ids = packed
        nearby = jnp.take(lap_round, nearby_ids, axis=0).reshape(7 * block_size, columns)
        return jnp.dot(block_ops[2].astype(jnp.float32), nearby.astype(jnp.float32), precision=lax.Precision.HIGHEST)
    lap_two = lax.map(second_block, (operators, neighbours))
    stepped = fields - advect_step * advect.reshape(nodes, nfield, levels) - hyper_rate * lap_two.reshape(nodes, nfield, levels)
    derivative = cheb_matrix(levels)
    slopes = jnp.einsum('nfj,ij->nfi', stepped, derivative, precision=lax.Precision.HIGHEST)
    fluxes = kappa_ref[None, None, :] * (1.0 + 0.5 * jnp.tanh(stepped)) * slopes
    diffused = stepped + radial_step * jnp.einsum('nfj,ij->nfi', fluxes, derivative, precision=lax.Precision.HIGHEST)
    flattened = diffused.reshape(nodes, columns)
    weighted = quad_weight[:, None] * flattened
    coeff = jnp.dot(basis.T, weighted, precision=lax.Precision.HIGHEST)
    modes = basis.shape[1]
    ratio = degree.astype(jnp.float32) / DEGMAX
    gain = 0.5 * jnp.sqrt(jnp.float32(modes) / nodes) * (1.0 - jnp.exp(-4.0 * ratio * ratio))
    removed = jnp.dot(basis, gain[:, None] * coeff, precision=lax.Precision.HIGHEST)
    return (flattened - removed).reshape(nodes, nfield, levels)
```

```python
import jax
import jax.numpy as jnp
import numpy as np
from jax import lax
from jax.experimental import pallas as pl
from jax.experimental.pallas import tpu as pltpu
from jax.sharding import PartitionSpec as P

DEGMAX = 22

advect_step = 0.25
hyper_rate = 0.1
radial_step = 0.25

BF = jnp.bfloat16
F32 = jnp.float32
VMEM = pl.BlockSpec(memory_space=pltpu.VMEM)
SMEM = pl.BlockSpec(memory_space=pltpu.SMEM)
PARAMS = pltpu.CompilerParams(vmem_limit_bytes=32 * 1024 * 1024)


def cheb_matrix(count):
    points = np.arange(count)
    angles = np.pi * points / (count - 1)
    upper, lower = angles[:, None], angles[None, :]
    spacing = -2.0 * np.sin((upper + lower) / 2.0) * np.sin((upper - lower) / 2.0)
    np.fill_diagonal(spacing, 1.0)
    weights = np.where((points == 0) | (points == count - 1), 2.0, 1.0)
    parity = np.where((upper * 0 + points[:, None] + points[None, :]) % 2 == 0, 1.0, -1.0)
    entries = weights[:, None] / weights[None, :] * parity / spacing
    np.fill_diagonal(entries, 0.0)
    matrix = entries - np.diag(entries.sum(axis=1))
    return (np.sin(angles)[:, None] * matrix / count).T.astype(np.float32)


def split(value):
    high = value.astype(BF)
    return high, (value - high.astype(F32)).astype(BF)


def dot(left, right):
    return jnp.dot(left, right, preferred_element_type=F32)


def dot3(left, right):
    return dot(left[0], right[0]) + (dot(left[0], right[1]) + dot(left[1], right[0]))


def call(kernel, outs, args, smem=0, scratch=()):
    return pl.pallas_call(
        kernel,
        out_shape=outs,
        in_specs=[SMEM] * smem + [VMEM] * (len(args) - smem),
        out_specs=jax.tree.map(lambda _: VMEM, outs),
        scratch_shapes=list(scratch),
        compiler_params=PARAMS,
    )(*args)


def shape(dims, kind):
    return jax.ShapeDtypeStruct(dims, kind)


def fill_window(window, low, own, high):
    rows = own.shape[0]
    window[0:rows] = low[...]
    window[rows : 2 * rows] = own[...]
    window[2 * rows : 3 * rows] = high[...]


def nearby(window, ids, b, block_size, near):
    parts = []
    for k in range(near):
        start = pl.multiple_of(ids[b, k] * block_size, block_size)
        parts.append(window[pl.ds(start, block_size), :])
    return jnp.concatenate(parts, axis=0)


def first_lap_kernel(ids, low, own, high, ops, lap, window):
    blocks, _, size, wide = ops.shape
    fill_window(window, low, own, high)
    for b in range(blocks):
        around = nearby(window, ids, b, size, wide // size)
        lap[b * size : (b + 1) * size] = dot(ops[b, 2], around).astype(BF)


def advect_kernel(ids, low, own, high, ops, fields, velocity, out, window):
    blocks, _, size, wide = ops.shape
    fill_window(window, low, own, high)
    for b in range(blocks):
        around = nearby(window, ids, b, size, wide // size)
        grad = dot(ops[b, 0:2].reshape(2 * size, wide), around)
        vel_x = velocity[pl.ds(2 * b * size, size, stride=2), :]
        vel_y = velocity[pl.ds(2 * b * size + 1, size, stride=2), :]
        rows = slice(b * size, (b + 1) * size)
        out[rows] = fields[rows] - advect_step * (vel_x * grad[:size] + vel_y * grad[size:])


def second_lap_kernel(ids, low, own, high, ops, part, stepped, narrow, window):
    blocks, _, size, wide = ops.shape
    fill_window(window, low, own, high)
    for b in range(blocks):
        around = nearby(window, ids, b, size, wide // size)
        rows = slice(b * size, (b + 1) * size)
        value = part[rows] - hyper_rate * dot(ops[b, 2], around)
        stepped[rows] = value
        narrow[rows] = value.astype(BF)


def prepare_kernel(basis, weight, gain, wbt_high, wbt_low, bg_high, bg_low):
    half = basis.shape[1] // 2
    high, low = split((basis[...] * weight[...]).T)
    wbt_high[...] = high
    wbt_low[...] = low
    for c in range(2):
        cols = slice(c * half, (c + 1) * half)
        high, low = split(basis[:, cols] * gain[:, cols])
        bg_high[c] = high
        bg_low[c] = low


def diffuse_kernel(count, place, *refs):
    shards = refs[:count]
    stepped, dh_high, dh_low, kappa, wbt_high, wbt_low, diffused, keep, send, levels = refs[count:]
    rad, core = place[0], place[1]
    nodes = stepped.shape[0]
    for d in range(count):
        levels[lax.rem(rad + count - d, count)] = shards[d][...]
    full_high = jnp.concatenate([dh_high[c] for c in range(count)], axis=1)
    full_low = jnp.concatenate([dh_low[c] for c in range(count)], axis=1)
    own = (dh_high[rad], dh_low[rad])
    step = nodes // 3
    for start in range(0, nodes, step):
        rows = slice(start, start + step)
        value = jnp.concatenate([levels[c, rows] for c in range(count)], axis=1)
        slopes = dot(value, full_high) + dot(value, full_low)
        fluxes = kappa[...] * (1.0 + 0.5 * jnp.tanh(value.astype(F32))) * slopes
        diffused[rows] = stepped[rows] + radial_step * dot3(split(fluxes), own)
    parts = split(diffused[...])
    half = keep.shape[0]
    for out, which in ((send, 1 - core), (keep, core)):
        rows = pl.ds(pl.multiple_of(which * half, half), half)
        out[...] = dot3((wbt_high[rows, :], wbt_low[rows, :]), parts)


def filter_kernel(place, diffused, mine, other, bg_high, bg_low, out):
    core = place[1]
    removed = dot3((bg_high[core], bg_low[core]), split(mine[...]))
    removed += dot3((bg_high[1 - core], bg_low[1 - core]), split(other[...]))
    out[...] = diffused[...] - removed


def shift(axis, by):
    count = lax.axis_size(axis)
    return [(i, (i + by) % count) for i in range(count)]


def halo(block):
    return lax.ppermute(block, "tile", shift("tile", 1)), lax.ppermute(block, "tile", shift("tile", -1))


def tile_sum(keep, send):
    count = lax.axis_size("tile")
    swap = [(i, i ^ 1) for i in range(count)]
    bits = [1 << k for k in range(1, count.bit_length() - 1)]
    mine = keep + lax.ppermute(send, "tile", swap)
    for k in range(len(bits)):
        pairs = [(i, i ^ bits[(k + i % 2) % len(bits)]) for i in range(count)]
        mine = mine + lax.ppermute(mine, "tile", pairs)
    return mine, lax.ppermute(mine, "tile", swap)


def body(fields, velocity, operators, neighbours, kappa_ref, quad_weight, basis, degree):
    nodes, nfield, levels = fields.shape
    blocks, _, size, _ = operators.shape
    modes = basis.shape[1]
    tiles, rads = lax.axis_size("tile"), lax.axis_size("rad")
    tile, rad = lax.axis_index("tile"), lax.axis_index("rad")
    fields = fields.reshape(nodes, levels)
    velocity = velocity.reshape(2 * nodes, levels)
    total = blocks * tiles
    ids = jnp.mod(neighbours - (tile - 1) * blocks + total, total)
    place = jnp.stack([rad, tile % 2])
    window = pltpu.VMEM((3 * nodes, levels), BF)

    ratio = degree.astype(F32) / DEGMAX
    gain = 0.5 * jnp.sqrt(F32(modes) / (nodes * tiles)) * (1.0 - jnp.exp(-4.0 * ratio * ratio))
    wbt_high, wbt_low, bg_high, bg_low = call(
        prepare_kernel,
        (shape((modes, nodes), BF),) * 2 + (shape((2, nodes, modes // 2), BF),) * 2,
        (basis, quad_weight[:, None], gain[None, :]),
    )
    dhat = cheb_matrix(rads * levels)
    dhat = np.stack([dhat[:, c * levels : (c + 1) * levels] for c in range(rads)])
    dh_high = dhat.astype(BF)
    dh_low = (dhat - dh_high.astype(np.float32)).astype(BF)

    rounded = fields.astype(BF)
    low, high = halo(rounded)
    lap = call(first_lap_kernel, shape((nodes, levels), BF), (ids, low, rounded, high, operators), 1, (window,))
    low_two, high_two = halo(lap)
    part = call(
        advect_kernel, shape((nodes, levels), F32), (ids, low, rounded, high, operators, fields, velocity), 1, (window,)
    )
    stepped, narrow = call(
        second_lap_kernel,
        (shape((nodes, levels), F32), shape((nodes, levels), BF)),
        (ids, low_two, lap, high_two, operators, part),
        1,
        (window,),
    )
    shards = [narrow] + [lax.ppermute(narrow, "rad", shift("rad", d)) for d in range(1, rads)]
    diffused, keep, send = call(
        lambda *refs: diffuse_kernel(rads, *refs),
        (shape((nodes, levels), F32),) + (shape((modes // 2, levels), F32),) * 2,
        (place, *shards, stepped, jnp.asarray(dh_high), jnp.asarray(dh_low), kappa_ref[None, :], wbt_high, wbt_low),
        1,
        (pltpu.VMEM((rads, nodes, levels), BF),),
    )
    mine, other = tile_sum(keep, send)
    filtered = call(
        filter_kernel, shape((nodes, levels), F32), (place, diffused, mine, other, bg_high, bg_low), 1
    )
    return filtered.reshape(nodes, nfield, levels)


def solution(mesh):
    return jax.shard_map(
        body,
        mesh=mesh,
        in_specs=(
            P("tile", None, "rad"),
            P("tile", None, "rad"),
            P("tile", None, None, None),
            P("tile", None),
            P(),
            P("tile"),
            P("tile", None),
            P(),
        ),
        out_specs=P("tile", None, "rad"),
        check_vma=False,
    )
```

```python
import jax
import jax.numpy as jnp
import numpy as np
from jax import lax
from jax.experimental import pallas as pl
from jax.experimental.pallas import tpu as pltpu
from jax.sharding import PartitionSpec as P

DEGMAX = 22

advect_step = 0.25
hyper_rate = 0.1
radial_step = 0.25

BF = jnp.bfloat16
F32 = jnp.float32
VMEM = pl.BlockSpec(memory_space=pltpu.VMEM)
SMEM = pl.BlockSpec(memory_space=pltpu.SMEM)
HBM = pl.BlockSpec(memory_space=pl.ANY)
PARAMS = pltpu.CompilerParams(vmem_limit_bytes=32 * 1024 * 1024)


def cheb_matrix(count):
    points = np.arange(count)
    angles = np.pi * points / (count - 1)
    upper, lower = angles[:, None], angles[None, :]
    spacing = -2.0 * np.sin((upper + lower) / 2.0) * np.sin((upper - lower) / 2.0)
    np.fill_diagonal(spacing, 1.0)
    weights = np.where((points == 0) | (points == count - 1), 2.0, 1.0)
    parity = np.where((upper * 0 + points[:, None] + points[None, :]) % 2 == 0, 1.0, -1.0)
    entries = weights[:, None] / weights[None, :] * parity / spacing
    np.fill_diagonal(entries, 0.0)
    matrix = entries - np.diag(entries.sum(axis=1))
    return (np.sin(angles)[:, None] * matrix / count).T.astype(np.float32)


def split(value):
    high = value.astype(BF)
    return high, (value - high.astype(F32)).astype(BF)


def dot(left, right):
    return jnp.dot(left, right, preferred_element_type=F32)


def dot3(left, right):
    wide = dot(left[0], jnp.concatenate(right, axis=1))
    count = right[0].shape[1]
    return wide[:, :count] + (wide[:, count:] + dot(left[1], right[0]))


def call(kernel, outs, args, spaces=None, scratch=()):
    return pl.pallas_call(
        kernel,
        out_shape=outs,
        in_specs=[{"s": SMEM, "h": HBM, "v": VMEM}[c] for c in spaces or "v" * len(args)],
        out_specs=jax.tree.map(lambda _: VMEM, outs),
        scratch_shapes=list(scratch),
        compiler_params=PARAMS,
    )(*args)


def shape(dims, kind):
    return jax.ShapeDtypeStruct(dims, kind)


def beside(dense, kind, first, count):
    return jnp.concatenate([dense[kind, first + s] for s in range(count)], axis=1)


def round_kernel(fields, wide, narrow, sems):
    parts = sems.shape[0]
    rows = wide.shape[0] // parts
    copies = []
    for p in range(parts):
        piece = pl.ds(p * rows, rows)
        copies.append(pltpu.make_async_copy(fields.at[piece], wide.at[piece], sems.at[p]))
        copies[-1].start()
    for p in range(parts):
        copies[p].wait()
        piece = slice(p * rows, (p + 1) * rows)
        narrow[piece] = wide[piece].astype(BF)


def prepare_kernel(ids, ops, basis, velocity, weight, gain, own, dense, lap_own, wbt_high, wbt_low, bg_high, bg_low,
                   vel, held, sems, op_sems):
    blocks, kinds, size, wide = ops.shape
    near = wide // size
    held_copy = pltpu.make_async_copy(basis, held, sems.at[0])
    held_copy.start()
    dense[...] = jnp.zeros(dense.shape, BF)
    total = blocks * lax.axis_size("tile")
    first = (lax.axis_index("tile") - 1) * blocks
    copies = []
    for b in range(blocks):
        for k in range(near):
            source = lax.rem(ids[b, k] - first + total, total)
            copies.append(
                pltpu.make_async_copy(
                    ops.at[b, :, :, pl.ds(k * size, size)],
                    dense.at[:, source, pl.ds(b * size, size), :],
                    op_sems.at[b, k],
                )
            )
            copies[-1].start()
    vel_copy = pltpu.make_async_copy(velocity, vel, sems.at[1])
    vel_copy.start()
    held_copy.wait()
    half = held.shape[1] // 2
    high, low = split(held[...].T * weight[...])
    wbt_high[...] = high
    wbt_low[...] = low
    for c in range(2):
        cols = slice(c * half, (c + 1) * half)
        high, low = split(held[:, cols] * gain[:, cols])
        bg_high[c] = high
        bg_low[c] = low
    for copy in copies:
        copy.wait()
    lap_own[...] = dot(beside(dense, 2, blocks, blocks), own[...])
    vel_copy.wait()


def first_lap_kernel(dense, lap_own, low, high, lap):
    blocks = dense.shape[1] // 3
    total = dot(beside(dense, 2, 0, blocks), low[...]) + dot(beside(dense, 2, 2 * blocks, blocks), high[...])
    lap[...] = (lap_own[...] + total).astype(BF)


def advect_kernel(dense, low, own, high, lap, fields, velocity, out):
    nodes = own.shape[0]
    blocks = dense.shape[1] // 3
    value = fields[...]
    for k in range(2):
        grad = dot(beside(dense, k, 0, blocks), low[...]) + dot(beside(dense, k, blocks, blocks), own[...])
        grad = grad + dot(beside(dense, k, 2 * blocks, blocks), high[...])
        value = value - advect_step * (velocity[pl.ds(k, nodes, stride=2), :] * grad)
    out[...] = value - hyper_rate * dot(beside(dense, 2, blocks, blocks), lap[...])


def second_lap_kernel(dense, low, high, part, stepped, narrow):
    blocks = dense.shape[1] // 3
    total = dot(beside(dense, 2, 0, blocks), low[...]) + dot(beside(dense, 2, 2 * blocks, blocks), high[...])
    value = part[...] - hyper_rate * total
    stepped[...] = value
    narrow[...] = value.astype(BF)


def project_kernel(wbt_high, wbt_low, value, out):
    out[...] = dot3((wbt_high[...], wbt_low[...]), split(value[...]))


def diffuse_kernel(count, *refs):
    shards = refs[:count]
    stepped, dh_high, dh_low, kappa, wbt_high, wbt_low, partial, diffused, keep, send, levels = refs[count:]
    rad, core = lax.axis_index("rad"), lax.rem(lax.axis_index("tile"), 2)
    for d in range(count):
        levels[lax.rem(rad + count - d, count)] = shards[d][...]
    value = jnp.concatenate([levels[c] for c in range(count)], axis=1)
    width = levels.shape[2]
    term = None
    group = 2 if count % 2 == 0 else 1
    for first in range(0, count, group):
        some = range(first, first + group)
        slopes = dot(value, jnp.concatenate([dh_high[c] for c in some], axis=1))
        slopes = slopes + dot(value, jnp.concatenate([dh_low[c] for c in some], axis=1))
        cols = slice(first * width, (first + group) * width)
        fluxes = kappa[:, cols] * (1.0 + 0.5 * jnp.tanh(value[:, cols].astype(F32))) * slopes
        more = dot3(split(fluxes), (dh_high[rad, cols, :], dh_low[rad, cols, :]))
        term = more if term is None else term + more
    term = radial_step * term
    diffused[...] = stepped[...] + term
    parts = split(term)
    half = keep.shape[0]
    for out, which in ((send, 1 - core), (keep, core)):
        rows = pl.ds(pl.multiple_of(which * half, half), half)
        out[...] = partial[rows, :] + dot3((wbt_high[rows, :], wbt_low[rows, :]), parts)


def filter_kernel(swap, value, modes, bg_high, bg_low, out):
    which = lax.rem(lax.axis_index("tile") + swap, 2)
    out[...] = value[...] - dot3((bg_high[which], bg_low[which]), split(modes[...]))


def shift(axis, by):
    count = lax.axis_size(axis)
    return [(i, (i + by) % count) for i in range(count)]


def halo(block):
    return lax.ppermute(block, "tile", shift("tile", 1)), lax.ppermute(block, "tile", shift("tile", -1))


def tile_sum(keep, send):
    count = lax.axis_size("tile")
    swap = [(i, i ^ 1) for i in range(count)]
    bits = [1 << k for k in range(1, count.bit_length() - 1)]
    mine = keep + lax.ppermute(send, "tile", swap)
    for k in range(len(bits)):
        pairs = [(i, i ^ bits[(k + i % 2) % len(bits)]) for i in range(count)]
        mine = mine + lax.ppermute(mine, "tile", pairs)
    return mine, lax.ppermute(mine, "tile", swap)


def body(fields, velocity, operators, neighbours, kappa_ref, quad_weight, basis, degree):
    nodes, nfield, levels = fields.shape
    blocks, _, size, _ = operators.shape
    modes = basis.shape[1]
    tiles, rads = lax.axis_size("tile"), lax.axis_size("rad")
    fields = fields.reshape(nodes, levels)
    velocity = velocity.reshape(2 * nodes, levels)
    wide = shape((nodes, levels), F32)
    thin = shape((nodes, levels), BF)

    ratio = degree.astype(F32) / DEGMAX
    gain = 0.5 * jnp.sqrt(F32(modes) / (nodes * tiles)) * (1.0 - jnp.exp(-4.0 * ratio * ratio))
    dhat = cheb_matrix(rads * levels)
    dhat = np.stack([dhat[:, c * levels : (c + 1) * levels] for c in range(rads)])
    dh_high = dhat.astype(BF)
    dh_low = (dhat - dh_high.astype(np.float32)).astype(BF)

    fields, rounded = call(round_kernel, (wide, thin), (fields,), "h", (pltpu.SemaphoreType.DMA((3,)),))
    low, high = halo(rounded)
    dense, lap_own, wbt_high, wbt_low, bg_high, bg_low, velocity = call(
        prepare_kernel,
        (shape((3, 3 * blocks, nodes, size), BF), wide)
        + (shape((modes, nodes), BF),) * 2
        + (shape((2, nodes, modes // 2), BF),) * 2
        + (shape((2 * nodes, levels), F32),),
        (neighbours, operators, basis, velocity, quad_weight[None, :], gain[None, :], rounded),
        "shhhvvv",
        (pltpu.VMEM((nodes, modes), F32), pltpu.SemaphoreType.DMA((2,)), pltpu.SemaphoreType.DMA(neighbours.shape)),
    )
    lap = call(first_lap_kernel, thin, (dense, lap_own, low, high))
    low_two, high_two = halo(lap)
    part = call(advect_kernel, wide, (dense, low, rounded, high, lap, fields, velocity))
    stepped, narrow = call(second_lap_kernel, (wide, thin), (dense, low_two, high_two, part))
    shards = [narrow] + [lax.ppermute(narrow, "rad", shift("rad", d)) for d in range(1, rads)]
    partial = call(project_kernel, shape((modes, levels), F32), (wbt_high, wbt_low, stepped))
    diffused, keep, send = call(
        lambda *refs: diffuse_kernel(rads, *refs),
        (wide,) + (shape((modes // 2, levels), F32),) * 2,
        (*shards, stepped, jnp.asarray(dh_high), jnp.asarray(dh_low), kappa_ref[None, :], wbt_high, wbt_low, partial),
        None,
        (pltpu.VMEM((rads, nodes, levels), BF),),
    )
    mine, other = tile_sum(keep, send)
    some = call(lambda *refs: filter_kernel(0, *refs), wide, (diffused, mine, bg_high, bg_low))
    filtered = call(lambda *refs: filter_kernel(1, *refs), wide, (some, other, bg_high, bg_low))
    return filtered.reshape(nodes, nfield, levels)


def solution(mesh):
    return jax.shard_map(
        body,
        mesh=mesh,
        in_specs=(
            P("tile", None, "rad"),
            P("tile", None, "rad"),
            P("tile", None, None, None),
            P("tile", None),
            P(),
            P("tile"),
            P("tile", None),
            P(),
        ),
        out_specs=P("tile", None, "rad"),
        check_vma=False,
    )
```

```python
import math

import jax
import jax.numpy as jnp
import numpy as np
from jax import lax
from jax.experimental import pallas as pl
from jax.experimental.pallas import tpu as pltpu
from jax.sharding import PartitionSpec as P

DEGMAX = 22

advect_step = 0.25
hyper_rate = 0.1
radial_step = 0.25

BF = jnp.bfloat16
F32 = jnp.float32
VMEM = pl.BlockSpec(memory_space=pltpu.VMEM)
SMEM = pl.BlockSpec(memory_space=pltpu.SMEM)
HBM = pl.BlockSpec(memory_space=pltpu.HBM)
PARAMS = pltpu.CompilerParams(vmem_limit_bytes=32 * 1024 * 1024)


def cheb_matrix(count):
    points = np.arange(count)
    angles = np.pi * points / (count - 1)
    upper, lower = angles[:, None], angles[None, :]
    spacing = -2.0 * np.sin((upper + lower) / 2.0) * np.sin((upper - lower) / 2.0)
    np.fill_diagonal(spacing, 1.0)
    weights = np.where((points == 0) | (points == count - 1), 2.0, 1.0)
    parity = np.where((upper * 0 + points[:, None] + points[None, :]) % 2 == 0, 1.0, -1.0)
    entries = weights[:, None] / weights[None, :] * parity / spacing
    np.fill_diagonal(entries, 0.0)
    matrix = entries - np.diag(entries.sum(axis=1))
    return (np.sin(angles)[:, None] * matrix / count).T.astype(np.float32)


def split(value):
    high = value.astype(BF)
    return high, (value - high.astype(F32)).astype(BF)


def dot(left, right):
    return jnp.dot(left, right, preferred_element_type=F32)


def dot3(left, right):
    wide = dot(left[0], jnp.concatenate(right, axis=1))
    count = right[0].shape[1]
    return wide[:, :count] + (wide[:, count:] + dot(left[1], right[0]))


def call(kernel, outs, args, spaces=None, scratch=()):
    return pl.pallas_call(
        kernel,
        out_shape=outs,
        in_specs=[{"s": SMEM, "h": HBM, "v": VMEM}[c] for c in spaces or "v" * len(args)],
        out_specs=jax.tree.map(lambda _: VMEM, outs),
        scratch_shapes=list(scratch),
        compiler_params=PARAMS,
    )(*args)


def shape(dims, kind):
    return jax.ShapeDtypeStruct(dims, kind)


def beside(dense, kind, first, count):
    return jnp.concatenate([dense[kind, first + s] for s in range(count)], axis=1)


def round_kernel(fields, wide, narrow, sems):
    parts = sems.shape[0]
    rows = wide.shape[0] // parts
    copies = []
    for p in range(parts):
        piece = pl.ds(p * rows, rows)
        copies.append(pltpu.make_async_copy(fields.at[piece], wide.at[piece], sems.at[p]))
        copies[-1].start()
    for p in range(parts):
        copies[p].wait()
        piece = slice(p * rows, (p + 1) * rows)
        narrow[piece] = wide[piece].astype(BF)


def prepare_kernel(ids, ops, basis, velocity, weight, degree, own, dense, lap_own, wbt_high, wbt_low, bg_high, bg_low,
                   vel, held, weight_held, degree_held, sems, op_sems):
    blocks, _, size, wide = ops.shape
    near = wide // size
    nodes, modes = held.shape
    pairs = ((basis, held), (weight, weight_held), (degree, degree_held), (velocity, vel))
    held_copies = [pltpu.make_async_copy(*pair, sems.at[k]) for k, pair in enumerate(pairs)]
    for copy in held_copies:
        copy.start()
    dense[...] = jnp.zeros(dense.shape, BF)
    total = blocks * lax.axis_size("tile")
    first = (lax.axis_index("tile") - 1) * blocks
    copies = []
    for b in range(blocks):
        for k in range(near):
            source = lax.rem(ids[b, k] - first + total, total)
            copies.append(
                pltpu.make_async_copy(
                    ops.at[b, :, :, pl.ds(k * size, size)],
                    dense.at[:, source, pl.ds(b * size, size), :],
                    op_sems.at[b, k],
                )
            )
            copies[-1].start()
    for copy in held_copies:
        copy.wait()
    ratio = degree_held[...].astype(F32) / DEGMAX
    gain = 0.5 * math.sqrt(modes / (nodes * lax.axis_size("tile"))) * (1.0 - jnp.exp(-4.0 * ratio * ratio))
    half = modes // 2
    high, low = split(held[...].T * weight_held[...])
    wbt_high[...] = high
    wbt_low[...] = low
    for c in range(2):
        cols = slice(c * half, (c + 1) * half)
        high, low = split(held[:, cols] * gain[:, cols])
        bg_high[c] = high
        bg_low[c] = low
    for copy in copies:
        copy.wait()
    lap_own[...] = dot(beside(dense, 2, blocks, blocks), own[...])


def first_lap_kernel(dense, lap_own, low, high, lap):
    blocks = dense.shape[1] // 3
    total = dot(beside(dense, 2, 0, blocks), low[...]) + dot(beside(dense, 2, 2 * blocks, blocks), high[...])
    lap[...] = (lap_own[...] + total).astype(BF)


def advect_kernel(dense, low, own, high, lap, fields, velocity, out):
    nodes = own.shape[0]
    blocks = dense.shape[1] // 3
    value = fields[...]
    for k in range(2):
        grad = dot(beside(dense, k, 0, blocks), low[...]) + dot(beside(dense, k, blocks, blocks), own[...])
        grad = grad + dot(beside(dense, k, 2 * blocks, blocks), high[...])
        value = value - advect_step * (velocity[pl.ds(k, nodes, stride=2), :] * grad)
    out[...] = value - hyper_rate * dot(beside(dense, 2, blocks, blocks), lap[...])


def second_lap_kernel(dense, low, high, part, stepped, narrow):
    blocks = dense.shape[1] // 3
    total = dot(beside(dense, 2, 0, blocks), low[...]) + dot(beside(dense, 2, 2 * blocks, blocks), high[...])
    value = part[...] - hyper_rate * total
    stepped[...] = value
    narrow[...] = value.astype(BF)


def project_kernel(wbt_high, wbt_low, value, out):
    out[...] = dot3((wbt_high[...], wbt_low[...]), split(value[...]))


def diffuse_kernel(count, *refs):
    shards = refs[:count]
    stepped, dh_high, dh_low, kappa, wbt_high, wbt_low, partial, diffused, keep, send, levels = refs[count:]
    rad, core = lax.axis_index("rad"), lax.rem(lax.axis_index("tile"), 2)
    for d in range(count):
        levels[lax.rem(rad + count - d, count)] = shards[d][...]
    value = jnp.concatenate([levels[c] for c in range(count)], axis=1)
    width = levels.shape[2]
    term = None
    group = 2 if count % 2 == 0 else 1
    for first in range(0, count, group):
        some = range(first, first + group)
        slopes = dot(value, jnp.concatenate([dh_high[c] for c in some], axis=1))
        slopes = slopes + dot(value, jnp.concatenate([dh_low[c] for c in some], axis=1))
        cols = slice(first * width, (first + group) * width)
        fluxes = kappa[:, cols] * (1.0 + 0.5 * jnp.tanh(value[:, cols].astype(F32))) * slopes
        more = dot3(split(fluxes), (dh_high[rad, cols, :], dh_low[rad, cols, :]))
        term = more if term is None else term + more
    term = radial_step * term
    diffused[...] = stepped[...] + term
    parts = split(term)
    half = keep.shape[0]
    for out, which in ((send, 1 - core), (keep, core)):
        rows = pl.ds(pl.multiple_of(which * half, half), half)
        out[...] = partial[rows, :] + dot3((wbt_high[rows, :], wbt_low[rows, :]), parts)


def filter_kernel(swap, value, modes, bg_high, bg_low, out):
    which = lax.rem(lax.axis_index("tile") + swap, 2)
    out[...] = value[...] - dot3((bg_high[which], bg_low[which]), split(modes[...]))


def shift(axis, by):
    count = lax.axis_size(axis)
    return [(i, (i + by) % count) for i in range(count)]


def halo(block):
    return lax.ppermute(block, "tile", shift("tile", 1)), lax.ppermute(block, "tile", shift("tile", -1))


def tile_sum(keep, send):
    count = lax.axis_size("tile")
    swap = [(i, i ^ 1) for i in range(count)]
    bits = [1 << k for k in range(1, count.bit_length() - 1)]
    mine = keep + lax.ppermute(send, "tile", swap)
    for k in range(len(bits)):
        pairs = [(i, i ^ bits[(k + i % 2) % len(bits)]) for i in range(count)]
        mine = mine + lax.ppermute(mine, "tile", pairs)
    return mine, lax.ppermute(mine, "tile", swap)


def body(fields, velocity, operators, neighbours, kappa_ref, quad_weight, basis, degree):
    nodes, nfield, levels = fields.shape
    blocks, _, size, _ = operators.shape
    modes = basis.shape[1]
    rads = lax.axis_size("rad")
    fields = fields.reshape(nodes, levels)
    velocity = velocity.reshape(2 * nodes, levels)
    wide = shape((nodes, levels), F32)
    thin = shape((nodes, levels), BF)

    dhat = cheb_matrix(rads * levels)
    dhat = np.stack([dhat[:, c * levels : (c + 1) * levels] for c in range(rads)])
    dh_high = dhat.astype(BF)
    dh_low = (dhat - dh_high.astype(np.float32)).astype(BF)

    fields, rounded = call(round_kernel, (wide, thin), (fields,), "h", (pltpu.SemaphoreType.DMA((3,)),))
    low, high = halo(rounded)
    dense, lap_own, wbt_high, wbt_low, bg_high, bg_low, velocity = call(
        prepare_kernel,
        (shape((3, 3 * blocks, nodes, size), BF), wide)
        + (shape((modes, nodes), BF),) * 2
        + (shape((2, nodes, modes // 2), BF),) * 2
        + (shape((2 * nodes, levels), F32),),
        (neighbours, operators, basis, velocity, quad_weight[None, :], degree[None, :], rounded),
        "shhhhhv",
        (
            pltpu.VMEM((nodes, modes), F32),
            pltpu.VMEM((1, nodes), F32),
            pltpu.VMEM((1, modes), jnp.int32),
            pltpu.SemaphoreType.DMA((4,)),
            pltpu.SemaphoreType.DMA(neighbours.shape),
        ),
    )
    lap = call(first_lap_kernel, thin, (dense, lap_own, low, high))
    low_two, high_two = halo(lap)
    part = call(advect_kernel, wide, (dense, low, rounded, high, lap, fields, velocity))
    stepped, narrow = call(second_lap_kernel, (wide, thin), (dense, low_two, high_two, part))
    shards = [narrow] + [lax.ppermute(narrow, "rad", shift("rad", d)) for d in range(1, rads)]
    partial = call(project_kernel, shape((modes, levels), F32), (wbt_high, wbt_low, stepped))
    diffused, keep, send = call(
        lambda *refs: diffuse_kernel(rads, *refs),
        (wide,) + (shape((modes // 2, levels), F32),) * 2,
        (*shards, stepped, jnp.asarray(dh_high), jnp.asarray(dh_low), kappa_ref[None, :], wbt_high, wbt_low, partial),
        None,
        (pltpu.VMEM((rads, nodes, levels), BF),),
    )
    mine, other = tile_sum(keep, send)
    some = call(lambda *refs: filter_kernel(0, *refs), wide, (diffused, mine, bg_high, bg_low))
    filtered = call(lambda *refs: filter_kernel(1, *refs), wide, (some, other, bg_high, bg_low))
    return filtered.reshape(nodes, nfield, levels)


def solution(mesh):
    return jax.shard_map(
        body,
        mesh=mesh,
        in_specs=(
            P("tile", None, "rad"),
            P("tile", None, "rad"),
            P("tile", None, None, None),
            P("tile", None),
            P(),
            P("tile"),
            P("tile", None),
            P(),
        ),
        out_specs=P("tile", None, "rad"),
        check_vma=False,
    )
```

```python
import math

import jax
import jax.numpy as jnp
import numpy as np
from jax import lax
from jax.experimental import pallas as pl
from jax.experimental.pallas import tpu as pltpu
from jax.sharding import PartitionSpec as P

DEGMAX = 22

advect_step = 0.25
hyper_rate = 0.1
radial_step = 0.25

BF = jnp.bfloat16
F32 = jnp.float32
VMEM = pl.BlockSpec(memory_space=pltpu.VMEM)
SMEM = pl.BlockSpec(memory_space=pltpu.SMEM)
HBM = pl.BlockSpec(memory_space=pltpu.HBM)
PARAMS = pltpu.CompilerParams(vmem_limit_bytes=32 * 1024 * 1024)


def cheb_matrix(count):
    points = np.arange(count)
    angles = np.pi * points / (count - 1)
    upper, lower = angles[:, None], angles[None, :]
    spacing = -2.0 * np.sin((upper + lower) / 2.0) * np.sin((upper - lower) / 2.0)
    np.fill_diagonal(spacing, 1.0)
    weights = np.where((points == 0) | (points == count - 1), 2.0, 1.0)
    parity = np.where((upper * 0 + points[:, None] + points[None, :]) % 2 == 0, 1.0, -1.0)
    entries = weights[:, None] / weights[None, :] * parity / spacing
    np.fill_diagonal(entries, 0.0)
    matrix = entries - np.diag(entries.sum(axis=1))
    return (np.sin(angles)[:, None] * matrix / count).T.astype(np.float32)


def split(value):
    high = value.astype(BF)
    return high, (value - high.astype(F32)).astype(BF)


def dot(left, right):
    return jnp.dot(left, right, preferred_element_type=F32)


def dot3(left, right):
    wide = dot(left[0], jnp.concatenate(right, axis=1))
    count = right[0].shape[1]
    return wide[:, :count] + (wide[:, count:] + dot(left[1], right[0]))


def call(kernel, outs, args, spaces=None, scratch=()):
    spaces = spaces or "v" * len(args)
    args = [pltpu.with_memory_space_constraint(a, pltpu.HBM) if c == "h" else a for a, c in zip(args, spaces)]
    return pl.pallas_call(
        kernel,
        out_shape=outs,
        in_specs=[{"s": SMEM, "h": HBM, "v": VMEM}[c] for c in spaces],
        out_specs=jax.tree.map(lambda _: VMEM, outs),
        scratch_shapes=list(scratch),
        compiler_params=PARAMS,
    )(*args)


def shape(dims, kind):
    return jax.ShapeDtypeStruct(dims, kind)


def beside(dense, kind, first, count):
    return jnp.concatenate([dense[kind, first + s] for s in range(count)], axis=1)


def round_kernel(fields, wide, narrow, sems):
    parts = sems.shape[0]
    rows = wide.shape[0] // parts
    copies = []
    for p in range(parts):
        piece = pl.ds(p * rows, rows)
        copies.append(pltpu.make_async_copy(fields.at[piece], wide.at[piece], sems.at[p]))
        copies[-1].start()
    for p in range(parts):
        copies[p].wait()
        piece = slice(p * rows, (p + 1) * rows)
        narrow[piece] = wide[piece].astype(BF)


def prepare_kernel(ids, ops, basis, velocity, weight, degree, own, dense, lap_own, wbt_high, wbt_low, bg_high, bg_low,
                   vel, held, weight_held, degree_held, sems, op_sems):
    blocks, _, size, wide = ops.shape
    near = wide // size
    nodes, modes = held.shape
    pairs = ((basis, held), (weight, weight_held), (degree, degree_held), (velocity, vel))
    held_copies = [pltpu.make_async_copy(*pair, sems.at[k]) for k, pair in enumerate(pairs)]
    for copy in held_copies:
        copy.start()
    dense[...] = jnp.zeros(dense.shape, BF)
    total = blocks * lax.axis_size("tile")
    first = (lax.axis_index("tile") - 1) * blocks
    copies = []
    for b in range(blocks):
        for k in range(near):
            source = lax.rem(ids[b, k] - first + total, total)
            copies.append(
                pltpu.make_async_copy(
                    ops.at[b, :, :, pl.ds(k * size, size)],
                    dense.at[:, source, pl.ds(b * size, size), :],
                    op_sems.at[b, k],
                )
            )
            copies[-1].start()
    for copy in held_copies:
        copy.wait()
    ratio = degree_held[...].astype(F32) / DEGMAX
    gain = 0.5 * math.sqrt(modes / (nodes * lax.axis_size("tile"))) * (1.0 - jnp.exp(-4.0 * ratio * ratio))
    half = modes // 2
    high, low = split(held[...].T * weight_held[...])
    wbt_high[...] = high
    wbt_low[...] = low
    for c in range(2):
        cols = slice(c * half, (c + 1) * half)
        high, low = split(held[:, cols] * gain[:, cols])
        bg_high[c] = high
        bg_low[c] = low
    for copy in copies:
        copy.wait()
    lap_own[...] = dot(beside(dense, 2, blocks, blocks), own[...])


def first_lap_kernel(dense, lap_own, low, high, lap):
    blocks = dense.shape[1] // 3
    total = dot(beside(dense, 2, 0, blocks), low[...]) + dot(beside(dense, 2, 2 * blocks, blocks), high[...])
    lap[...] = (lap_own[...] + total).astype(BF)


def advect_kernel(dense, low, own, high, lap, fields, velocity, out):
    nodes = own.shape[0]
    blocks = dense.shape[1] // 3
    value = fields[...]
    for k in range(2):
        grad = dot(beside(dense, k, 0, blocks), low[...]) + dot(beside(dense, k, blocks, blocks), own[...])
        grad = grad + dot(beside(dense, k, 2 * blocks, blocks), high[...])
        value = value - advect_step * (velocity[pl.ds(k, nodes, stride=2), :] * grad)
    out[...] = value - hyper_rate * dot(beside(dense, 2, blocks, blocks), lap[...])


def second_lap_kernel(dense, low, high, part, stepped, narrow):
    blocks = dense.shape[1] // 3
    total = dot(beside(dense, 2, 0, blocks), low[...]) + dot(beside(dense, 2, 2 * blocks, blocks), high[...])
    value = part[...] - hyper_rate * total
    stepped[...] = value
    narrow[...] = value.astype(BF)


def project_kernel(wbt_high, wbt_low, value, out):
    out[...] = dot3((wbt_high[...], wbt_low[...]), split(value[...]))


def diffuse_kernel(count, *refs):
    shards = refs[:count]
    stepped, dh_high, dh_low, kappa, wbt_high, wbt_low, partial, diffused, keep, send, levels = refs[count:]
    rad, core = lax.axis_index("rad"), lax.rem(lax.axis_index("tile"), 2)
    for d in range(count):
        levels[lax.rem(rad + count - d, count)] = shards[d][...]
    value = jnp.concatenate([levels[c] for c in range(count)], axis=1)
    width = levels.shape[2]
    term = None
    group = 2 if count % 2 == 0 else 1
    for first in range(0, count, group):
        some = range(first, first + group)
        slopes = dot(value, jnp.concatenate([dh_high[c] for c in some], axis=1))
        slopes = slopes + dot(value, jnp.concatenate([dh_low[c] for c in some], axis=1))
        cols = slice(first * width, (first + group) * width)
        fluxes = kappa[:, cols] * (1.0 + 0.5 * jnp.tanh(value[:, cols].astype(F32))) * slopes
        more = dot3(split(fluxes), (dh_high[rad, cols, :], dh_low[rad, cols, :]))
        term = more if term is None else term + more
    term = radial_step * term
    diffused[...] = stepped[...] + term
    parts = split(term)
    half = keep.shape[0]
    for out, which in ((send, 1 - core), (keep, core)):
        rows = pl.ds(pl.multiple_of(which * half, half), half)
        out[...] = partial[rows, :] + dot3((wbt_high[rows, :], wbt_low[rows, :]), parts)


def filter_kernel(swap, value, modes, bg_high, bg_low, out):
    which = lax.rem(lax.axis_index("tile") + swap, 2)
    out[...] = value[...] - dot3((bg_high[which], bg_low[which]), split(modes[...]))


def shift(axis, by):
    count = lax.axis_size(axis)
    return [(i, (i + by) % count) for i in range(count)]


def halo(block):
    return lax.ppermute(block, "tile", shift("tile", 1)), lax.ppermute(block, "tile", shift("tile", -1))


def tile_sum(keep, send):
    count = lax.axis_size("tile")
    swap = [(i, i ^ 1) for i in range(count)]
    bits = [1 << k for k in range(1, count.bit_length() - 1)]
    mine = keep + lax.ppermute(send, "tile", swap)
    for k in range(len(bits)):
        pairs = [(i, i ^ bits[(k + i % 2) % len(bits)]) for i in range(count)]
        mine = mine + lax.ppermute(mine, "tile", pairs)
    return mine, lax.ppermute(mine, "tile", swap)


def body(fields, velocity, operators, neighbours, kappa_ref, quad_weight, basis, degree):
    nodes, nfield, levels = fields.shape
    blocks, _, size, _ = operators.shape
    modes = basis.shape[1]
    rads = lax.axis_size("rad")
    fields = fields.reshape(nodes, levels)
    velocity = velocity.reshape(2 * nodes, levels)
    wide = shape((nodes, levels), F32)
    thin = shape((nodes, levels), BF)

    dhat = cheb_matrix(rads * levels)
    dhat = np.stack([dhat[:, c * levels : (c + 1) * levels] for c in range(rads)])
    dh_high = dhat.astype(BF)
    dh_low = (dhat - dh_high.astype(np.float32)).astype(BF)

    fields, rounded = call(round_kernel, (wide, thin), (fields,), "h", (pltpu.SemaphoreType.DMA((3,)),))
    low, high = halo(rounded)
    dense, lap_own, wbt_high, wbt_low, bg_high, bg_low, velocity = call(
        prepare_kernel,
        (shape((3, 3 * blocks, nodes, size), BF), wide)
        + (shape((modes, nodes), BF),) * 2
        + (shape((2, nodes, modes // 2), BF),) * 2
        + (shape((2 * nodes, levels), F32),),
        (neighbours, operators, basis, velocity, quad_weight[None, :], degree[None, :], rounded),
        "shhhhhv",
        (
            pltpu.VMEM((nodes, modes), F32),
            pltpu.VMEM((1, nodes), F32),
            pltpu.VMEM((1, modes), jnp.int32),
            pltpu.SemaphoreType.DMA((4,)),
            pltpu.SemaphoreType.DMA(neighbours.shape),
        ),
    )
    lap = call(first_lap_kernel, thin, (dense, lap_own, low, high))
    low_two, high_two = halo(lap)
    part = call(advect_kernel, wide, (dense, low, rounded, high, lap, fields, velocity))
    stepped, narrow = call(second_lap_kernel, (wide, thin), (dense, low_two, high_two, part))
    shards = [narrow] + [lax.ppermute(narrow, "rad", shift("rad", d)) for d in range(1, rads)]
    partial = call(project_kernel, shape((modes, levels), F32), (wbt_high, wbt_low, stepped))
    diffused, keep, send = call(
        lambda *refs: diffuse_kernel(rads, *refs),
        (wide,) + (shape((modes // 2, levels), F32),) * 2,
        (*shards, stepped, jnp.asarray(dh_high), jnp.asarray(dh_low), kappa_ref[None, :], wbt_high, wbt_low, partial),
        None,
        (pltpu.VMEM((rads, nodes, levels), BF),),
    )
    mine, other = tile_sum(keep, send)
    some = call(lambda *refs: filter_kernel(0, *refs), wide, (diffused, mine, bg_high, bg_low))
    filtered = call(lambda *refs: filter_kernel(1, *refs), wide, (some, other, bg_high, bg_low))
    return filtered.reshape(nodes, nfield, levels)


def solution(mesh):
    return jax.shard_map(
        body,
        mesh=mesh,
        in_specs=(
            P("tile", None, "rad"),
            P("tile", None, "rad"),
            P("tile", None, None, None),
            P("tile", None),
            P(),
            P("tile"),
            P("tile", None),
            P(),
        ),
        out_specs=P("tile", None, "rad"),
        check_vma=False,
    )
```

```python
import math

import jax
import jax.numpy as jnp
import numpy as np
from jax import lax
from jax.experimental import pallas as pl
from jax.experimental.pallas import tpu as pltpu
from jax.sharding import PartitionSpec as P

DEGMAX = 22

advect_step = 0.25
hyper_rate = 0.1
radial_step = 0.25

BF = jnp.bfloat16
F32 = jnp.float32
VMEM = pl.BlockSpec(memory_space=pltpu.VMEM)
SMEM = pl.BlockSpec(memory_space=pltpu.SMEM)
HBM = pl.BlockSpec(memory_space=pltpu.HBM)
PARAMS = pltpu.CompilerParams(vmem_limit_bytes=32 * 1024 * 1024)


def cheb_matrix(count):
    points = np.arange(count)
    angles = np.pi * points / (count - 1)
    upper, lower = angles[:, None], angles[None, :]
    spacing = -2.0 * np.sin((upper + lower) / 2.0) * np.sin((upper - lower) / 2.0)
    np.fill_diagonal(spacing, 1.0)
    weights = np.where((points == 0) | (points == count - 1), 2.0, 1.0)
    parity = np.where((upper * 0 + points[:, None] + points[None, :]) % 2 == 0, 1.0, -1.0)
    entries = weights[:, None] / weights[None, :] * parity / spacing
    np.fill_diagonal(entries, 0.0)
    matrix = entries - np.diag(entries.sum(axis=1))
    return (np.sin(angles)[:, None] * matrix / count).T.astype(np.float32)


def split(value):
    high = value.astype(BF)
    return high, (value - high.astype(F32)).astype(BF)


def dot(left, right):
    return jnp.dot(left, right, preferred_element_type=F32)


def dot3(left, right):
    wide = dot(left[0], jnp.concatenate(right, axis=1))
    count = right[0].shape[1]
    return wide[:, :count] + (wide[:, count:] + dot(left[1], right[0]))


def call(kernel, outs, args, spaces=None, scratch=()):
    spaces = spaces or "v" * len(args)
    args = [pltpu.with_memory_space_constraint(a, pltpu.HBM) if c == "h" else a for a, c in zip(args, spaces)]
    return pl.pallas_call(
        kernel,
        out_shape=outs,
        in_specs=[{"s": SMEM, "h": HBM, "v": VMEM}[c] for c in spaces],
        out_specs=jax.tree.map(lambda _: VMEM, outs),
        scratch_shapes=list(scratch),
        compiler_params=PARAMS,
    )(*args)


def shape(dims, kind):
    return jax.ShapeDtypeStruct(dims, kind)


def beside(dense, first, count):
    return jnp.concatenate([dense[first + s] for s in range(count)], axis=1)


def stencil_copies(ids, ops, kinds, dense, sems):
    blocks, _, size, wide = ops.shape
    total = blocks * lax.axis_size("tile")
    first = (lax.axis_index("tile") - 1) * blocks
    dense[...] = jnp.zeros(dense.shape, BF)
    copies = []
    for b in range(blocks):
        for k in range(wide // size):
            source = lax.rem(ids[b, k] - first + total, total)
            copy = pltpu.make_async_copy(
                ops.at[b, kinds, :, pl.ds(k * size, size)],
                dense.at[:, source, pl.ds(b * size, size), :],
                sems.at[b, k],
            )
            copy.start()
            copies.append(copy)
    return copies


def round_kernel(fields, neighbours, wide, narrow, ids, sems, ids_sem):
    parts = sems.shape[0]
    rows = wide.shape[0] // parts
    copies = []
    for p in range(parts):
        piece = pl.ds(p * rows, rows)
        copies.append(pltpu.make_async_copy(fields.at[piece], wide.at[piece], sems.at[p]))
        copies[-1].start()
    ids_copy = pltpu.make_async_copy(neighbours, ids, ids_sem)
    ids_copy.start()
    for p in range(parts):
        copies[p].wait()
        piece = slice(p * rows, (p + 1) * rows)
        narrow[piece] = wide[piece].astype(BF)
    ids_copy.wait()


def prepare_kernel(ids, ops, own, dense, lap_own, sems):
    blocks = ops.shape[0]
    for copy in stencil_copies(ids, ops, pl.ds(2, 1), dense, sems):
        copy.wait()
    lap_own[...] = dot(beside(dense.at[0], blocks, blocks), own[...])


def around(dense, low, high):
    blocks = dense.shape[0] // 3
    return dot(beside(dense, 0, blocks), low[...]) + dot(beside(dense, 2 * blocks, blocks), high[...])


def first_lap_kernel(dense, lap_own, low, high, lap):
    lap[...] = (lap_own[...] + around(dense.at[0], low, high)).astype(BF)


def advect_kernel(ids, ops, velocity, basis, weight, degree, lap_dense, low, own, high, lap, fields,
                  out, wbt_high, wbt_low, bg_high, bg_low, dense, vel, held, weight_held, degree_held, sems, op_sems):
    blocks = ops.shape[0]
    nodes, modes = held.shape
    pairs = ((basis, held), (weight, weight_held), (degree, degree_held), (velocity, vel))
    held_copies = [pltpu.make_async_copy(*pair, sems.at[k]) for k, pair in enumerate(pairs)]
    for copy in held_copies:
        copy.start()
    copies = stencil_copies(ids, ops, pl.ds(0, 2), dense, op_sems)
    for copy in held_copies:
        copy.wait()
    ratio = degree_held[...].astype(F32) / DEGMAX
    gain = 0.5 * math.sqrt(modes / (nodes * lax.axis_size("tile"))) * (1.0 - jnp.exp(-4.0 * ratio * ratio))
    half = modes // 2
    for c in range(2):
        cols = slice(c * half, (c + 1) * half)
        high_part, low_part = split(held[:, cols] * gain[:, cols])
        bg_high[c] = high_part
        bg_low[c] = low_part
    high_part, low_part = split(held[...].T * weight_held[...])
    wbt_high[...] = high_part
    wbt_low[...] = low_part
    for copy in copies:
        copy.wait()
    value = fields[...] - hyper_rate * dot(beside(lap_dense.at[0], blocks, blocks), lap[...])
    for k in range(2):
        grad = dot(beside(dense.at[k], blocks, blocks), own[...]) + around(dense.at[k], low, high)
        value = value - advect_step * (vel[pl.ds(k, nodes, stride=2), :] * grad)
    out[...] = value


def second_lap_kernel(dense, low, high, part, stepped, narrow):
    value = part[...] - hyper_rate * around(dense.at[0], low, high)
    stepped[...] = value
    narrow[...] = value.astype(BF)


def project_kernel(wbt_high, wbt_low, value, out):
    out[...] = dot3((wbt_high[...], wbt_low[...]), split(value[...]))


def diffuse_kernel(count, *refs):
    shards = refs[:count]
    stepped, dh_high, dh_low, kappa, wbt, early, diffused, keep, send = refs[count:]
    rad, core = lax.axis_index("rad"), lax.rem(lax.axis_index("tile"), 2)
    width = stepped.shape[1]
    chunk = [lax.rem(rad + count - d, count) for d in range(count)]
    rows = [pl.ds(pl.multiple_of(c * width, width), width) for c in chunk]
    value = jnp.concatenate([shard[...] for shard in shards], axis=1)
    term = None
    group = 2 if count % 2 == 0 else 1
    for first in range(0, count, group):
        some = range(first, first + group)
        slopes = None
        for table in (dh_high, dh_low):
            weights = [jnp.concatenate([table[chunk[i], rows[j], :] for j in range(count)], axis=0) for i in some]
            more = dot(value, jnp.concatenate(weights, axis=1))
            slopes = more if slopes is None else slopes + more
        rate = jnp.concatenate([kappa[chunk[i]] for i in some], axis=1)
        bend = jnp.tanh(value[:, first * width : (first + group) * width].astype(F32))
        fluxes = (rate + (0.5 * rate) * bend) * slopes
        own = [jnp.concatenate([table[rad, rows[i], :] for i in some], axis=0) for table in (dh_high, dh_low)]
        more = dot3(split(fluxes), own)
        term = more if term is None else term + more
    term = radial_step * term
    diffused[...] = stepped[...] + term
    late = jnp.concatenate(split(term), axis=1)
    half = keep.shape[0]
    for out, which in ((send, 1 - core), (keep, core)):
        modes = pl.ds(pl.multiple_of(which * half, half), half)
        total = dot(wbt[modes, :], late)
        out[...] = early[modes, :] + total[:, :width] + total[:, width:]


def filter_kernel(swap, value, modes, bg_high, bg_low, out):
    which = lax.rem(lax.axis_index("tile") + swap, 2)
    out[...] = value[...] - dot3((bg_high[which], bg_low[which]), split(modes[...]))


def shift(axis, by):
    count = lax.axis_size(axis)
    return [(i, (i + by) % count) for i in range(count)]


def halo(block):
    return lax.ppermute(block, "tile", shift("tile", 1)), lax.ppermute(block, "tile", shift("tile", -1))


def swap(block):
    return lax.ppermute(block, "tile", [(i, i ^ 1) for i in range(lax.axis_size("tile"))])


def chip_sum(block):
    count = lax.axis_size("tile")
    bits = [1 << k for k in range(1, count.bit_length() - 1)]
    for k in range(len(bits)):
        pairs = [(i, i ^ bits[(k + i % 2) % len(bits)]) for i in range(count)]
        block = block + lax.ppermute(block, "tile", pairs)
    return block


def body(fields, velocity, operators, neighbours, kappa_ref, quad_weight, basis, degree):
    nodes, nfield, levels = fields.shape
    blocks, _, size, _ = operators.shape
    modes = basis.shape[1]
    rads = lax.axis_size("rad")
    fields = fields.reshape(nodes, levels)
    velocity = velocity.reshape(2 * nodes, levels)
    wide = shape((nodes, levels), F32)
    thin = shape((nodes, levels), BF)

    dhat = cheb_matrix(rads * levels)
    dhat = np.stack([dhat[:, c * levels : (c + 1) * levels] for c in range(rads)])
    dh_high = dhat.astype(BF)
    dh_low = (dhat - dh_high.astype(np.float32)).astype(BF)

    half = shape((modes // 2, levels), F32)
    dma = pltpu.SemaphoreType.DMA
    fields, rounded, ids = call(
        round_kernel,
        (wide, thin, shape(neighbours.shape, neighbours.dtype)),
        (fields, neighbours),
        "hh",
        (dma((3,)), dma(())),
    )
    low, high = halo(rounded)
    lap_dense, lap_own = call(
        prepare_kernel,
        (shape((1, 3 * blocks, nodes, size), BF), wide),
        (ids, operators, rounded),
        "shv",
        (dma(neighbours.shape),),
    )
    lap = call(first_lap_kernel, thin, (lap_dense, lap_own, low, high))
    low_two, high_two = halo(lap)
    part, wbt_high, wbt_low, bg_high, bg_low = call(
        advect_kernel,
        (wide,) + (shape((modes, nodes), BF),) * 2 + (shape((2, nodes, modes // 2), BF),) * 2,
        (ids, operators, velocity, basis, quad_weight[None, :], degree[None, :])
        + (lap_dense, low, rounded, high, lap, fields),
        "shhhhhvvvvvv",
        (
            pltpu.VMEM((2, 3 * blocks, nodes, size), BF),
            pltpu.VMEM((2 * nodes, levels), F32),
            pltpu.VMEM((nodes, modes), F32),
            pltpu.VMEM((1, nodes), F32),
            pltpu.VMEM((1, modes), jnp.int32),
            dma((4,)),
            dma(neighbours.shape),
        ),
    )
    stepped, narrow = call(second_lap_kernel, (wide, thin), (lap_dense, low_two, high_two, part))
    shards = [narrow] + [lax.ppermute(narrow, "rad", shift("rad", d)) for d in range(1, rads)]
    early = call(project_kernel, shape((modes, levels), F32), (wbt_high, wbt_low, stepped))
    diffused, keep, send = call(
        lambda *refs: diffuse_kernel(rads, *refs),
        (wide, half, half),
        (*shards, stepped, jnp.asarray(dh_high), jnp.asarray(dh_low), kappa_ref.reshape(rads, 1, levels))
        + (wbt_high, early),
    )
    mine = chip_sum(keep + swap(send))
    other = swap(mine)
    some = call(lambda *refs: filter_kernel(0, *refs), wide, (diffused, mine, bg_high, bg_low))
    filtered = call(lambda *refs: filter_kernel(1, *refs), wide, (some, other, bg_high, bg_low))
    return filtered.reshape(nodes, nfield, levels)


def solution(mesh):
    return jax.shard_map(
        body,
        mesh=mesh,
        in_specs=(
            P("tile", None, "rad"),
            P("tile", None, "rad"),
            P("tile", None, None, None),
            P("tile", None),
            P(),
            P("tile"),
            P("tile", None),
            P(),
        ),
        out_specs=P("tile", None, "rad"),
        check_vma=False,
    )
```

```python
import math

import jax
import jax.numpy as jnp
import numpy as np
from jax import lax
from jax.experimental import pallas as pl
from jax.experimental.pallas import tpu as pltpu
from jax.sharding import PartitionSpec as P

DEGMAX = 22

advect_step = 0.25
hyper_rate = 0.1
radial_step = 0.25

BF = jnp.bfloat16
F32 = jnp.float32
VMEM = pl.BlockSpec(memory_space=pltpu.VMEM)
SMEM = pl.BlockSpec(memory_space=pltpu.SMEM)
HBM = pl.BlockSpec(memory_space=pltpu.HBM)
PARAMS = pltpu.CompilerParams(vmem_limit_bytes=32 * 1024 * 1024)


def cheb_matrix(count):
    points = np.arange(count)
    angles = np.pi * points / (count - 1)
    upper, lower = angles[:, None], angles[None, :]
    spacing = -2.0 * np.sin((upper + lower) / 2.0) * np.sin((upper - lower) / 2.0)
    np.fill_diagonal(spacing, 1.0)
    weights = np.where((points == 0) | (points == count - 1), 2.0, 1.0)
    parity = np.where((upper * 0 + points[:, None] + points[None, :]) % 2 == 0, 1.0, -1.0)
    entries = weights[:, None] / weights[None, :] * parity / spacing
    np.fill_diagonal(entries, 0.0)
    matrix = entries - np.diag(entries.sum(axis=1))
    return (np.sin(angles)[:, None] * matrix / count).T.astype(np.float32)


def split(value):
    high = value.astype(BF)
    return high, (value - high.astype(F32)).astype(BF)


def dot(left, right):
    return jnp.dot(left, right, preferred_element_type=F32)


def dot3(left, right):
    wide = dot(left[0], jnp.concatenate(right, axis=1))
    count = right[0].shape[1]
    return wide[:, :count] + (wide[:, count:] + dot(left[1], right[0]))


def call(kernel, outs, args, spaces=None, scratch=()):
    spaces = spaces or "v" * len(args)
    args = [pltpu.with_memory_space_constraint(a, pltpu.HBM) if c == "h" else a for a, c in zip(args, spaces)]
    return pl.pallas_call(
        kernel,
        out_shape=outs,
        in_specs=[{"s": SMEM, "h": HBM, "v": VMEM}[c] for c in spaces],
        out_specs=jax.tree.map(lambda _: VMEM, outs),
        scratch_shapes=list(scratch),
        compiler_params=PARAMS,
    )(*args)


def shape(dims, kind):
    return jax.ShapeDtypeStruct(dims, kind)


def beside(dense, first, count):
    return jnp.concatenate([dense[first + s] for s in range(count)], axis=1)


def stencil_copies(ids, ops, kinds, dense, sems):
    blocks, _, size, wide = ops.shape
    total = blocks * lax.axis_size("tile")
    first = (lax.axis_index("tile") - 1) * blocks
    dense[...] = jnp.zeros(dense.shape, BF)
    copies = []
    for b in range(blocks):
        for k in range(wide // size):
            source = lax.rem(ids[b, k] - first + total, total)
            copy = pltpu.make_async_copy(
                ops.at[b, kinds, :, pl.ds(k * size, size)],
                dense.at[:, source, pl.ds(b * size, size), :],
                sems.at[b, k],
            )
            copy.start()
            copies.append(copy)
    return copies


def round_kernel(fields, neighbours, wide, narrow, ids, sems, ids_sem):
    parts = sems.shape[0]
    rows = wide.shape[0] // parts
    copies = []
    for p in range(parts):
        piece = pl.ds(p * rows, rows)
        copies.append(pltpu.make_async_copy(fields.at[piece], wide.at[piece], sems.at[p]))
        copies[-1].start()
    ids_copy = pltpu.make_async_copy(neighbours, ids, ids_sem)
    ids_copy.start()
    for p in range(parts):
        copies[p].wait()
        piece = slice(p * rows, (p + 1) * rows)
        narrow[piece] = wide[piece].astype(BF)
    ids_copy.wait()


def prepare_kernel(ids, ops, own, dense, lap_own, sems):
    blocks = ops.shape[0]
    for copy in stencil_copies(ids, ops, pl.ds(2, 1), dense, sems):
        copy.wait()
    lap_own[...] = dot(beside(dense.at[0], blocks, blocks), own[...])


def around(dense, low, high):
    blocks = dense.shape[0] // 3
    return dot(beside(dense, 0, blocks), low[...]) + dot(beside(dense, 2 * blocks, blocks), high[...])


def first_lap_kernel(dense, lap_own, low, high, lap):
    lap[...] = (lap_own[...] + around(dense.at[0], low, high)).astype(BF)


def advect_kernel(ids, ops, velocity, lap_dense, low, own, high, lap, fields, out, dense, vel, vel_sem, op_sems):
    blocks = ops.shape[0]
    nodes = own.shape[0]
    vel_copy = pltpu.make_async_copy(velocity, vel, vel_sem)
    vel_copy.start()
    copies = stencil_copies(ids, ops, pl.ds(0, 2), dense, op_sems)
    value = fields[...] - hyper_rate * dot(beside(lap_dense.at[0], blocks, blocks), lap[...])
    vel_copy.wait()
    for copy in copies:
        copy.wait()
    for k in range(2):
        grad = dot(beside(dense.at[k], blocks, blocks), own[...]) + around(dense.at[k], low, high)
        value = value - advect_step * (vel[pl.ds(k, nodes, stride=2), :] * grad)
    out[...] = value


def second_lap_kernel(dense, low, high, part, stepped, narrow):
    value = part[...] - hyper_rate * around(dense.at[0], low, high)
    stepped[...] = value
    narrow[...] = value.astype(BF)


def project_kernel(basis, weight, degree, value, wbt, early, bg_high, bg_low, held, weight_held, degree_held, sems):
    nodes, modes = held.shape
    pairs = ((basis, held), (weight, weight_held), (degree, degree_held))
    copies = [pltpu.make_async_copy(*pair, sems.at[k]) for k, pair in enumerate(pairs)]
    for copy in copies:
        copy.start()
    for copy in copies:
        copy.wait()
    parts = split(held[...].T * weight_held[...])
    wbt[...] = parts[0]
    early[...] = dot3(parts, split(value[...]))
    ratio = degree_held[...].astype(F32) / DEGMAX
    gain = 0.5 * math.sqrt(modes / (nodes * lax.axis_size("tile"))) * (1.0 - jnp.exp(-4.0 * ratio * ratio))
    half = modes // 2
    for c in range(2):
        cols = slice(c * half, (c + 1) * half)
        bg_high[c], bg_low[c] = split(held[:, cols] * gain[:, cols])


def diffuse_kernel(count, *refs):
    shards = refs[:count]
    stepped, dh_high, dh_low, kappa, wbt, early, diffused, keep, send = refs[count:]
    rad, core = lax.axis_index("rad"), lax.rem(lax.axis_index("tile"), 2)
    width = stepped.shape[1]
    chunk = [lax.rem(rad + count - d, count) for d in range(count)]
    rows = [pl.ds(pl.multiple_of(c * width, width), width) for c in chunk]
    value = jnp.concatenate([shard[...] for shard in shards], axis=1)
    term = None
    group = 2 if count % 2 == 0 else 1
    for first in range(0, count, group):
        some = range(first, first + group)
        slopes = None
        for table in (dh_high, dh_low):
            weights = [jnp.concatenate([table[chunk[i], rows[j], :] for j in range(count)], axis=0) for i in some]
            more = dot(value, jnp.concatenate(weights, axis=1))
            slopes = more if slopes is None else slopes + more
        rate = jnp.concatenate([kappa[chunk[i]] for i in some], axis=1)
        bend = jnp.tanh(value[:, first * width : (first + group) * width].astype(F32))
        fluxes = (rate + (0.5 * rate) * bend) * slopes
        own = [jnp.concatenate([table[rad, rows[i], :] for i in some], axis=0) for table in (dh_high, dh_low)]
        more = dot3(split(fluxes), own)
        term = more if term is None else term + more
    term = radial_step * term
    diffused[...] = stepped[...] + term
    late = jnp.concatenate(split(term), axis=1)
    half = keep.shape[0]
    for out, which in ((send, 1 - core), (keep, core)):
        modes = pl.ds(pl.multiple_of(which * half, half), half)
        total = dot(wbt[modes, :], late)
        out[...] = early[modes, :] + total[:, :width] + total[:, width:]


def filter_kernel(swap, value, modes, bg_high, bg_low, out):
    which = lax.rem(lax.axis_index("tile") + swap, 2)
    out[...] = value[...] - dot3((bg_high[which], bg_low[which]), split(modes[...]))


def shift(axis, by):
    count = lax.axis_size(axis)
    return [(i, (i + by) % count) for i in range(count)]


def halo(block):
    return lax.ppermute(block, "tile", shift("tile", 1)), lax.ppermute(block, "tile", shift("tile", -1))


def swap(block):
    return lax.ppermute(block, "tile", [(i, i ^ 1) for i in range(lax.axis_size("tile"))])


def packed(block):
    top = jnp.max(jnp.abs(block), keepdims=True)
    power = jnp.round(jnp.log2(jnp.maximum(top, 1e-30)))
    tail = jnp.broadcast_to(power, (16, block.shape[1]))
    return jnp.concatenate([block * jnp.exp2(8.0 - power), tail], axis=0).astype(jnp.float16)


def unpacked(sent):
    rows = sent.shape[0] - 16
    return sent[:rows].astype(F32) * jnp.exp2(sent[rows : rows + 1].astype(F32) - 8.0)


def chip_sum(block):
    count = lax.axis_size("tile")
    if count <= 8:
        sent = packed(block)
        parts = [lax.ppermute(sent, "tile", [(i, i ^ m) for i in range(count)]) for m in range(2, count, 2)]
        return sum((unpacked(part) for part in parts), block)
    for m in [1 << k for k in range(1, count.bit_length() - 1)]:
        block = block + lax.ppermute(block, "tile", [(i, i ^ m) for i in range(count)])
    return block


def body(fields, velocity, operators, neighbours, kappa_ref, quad_weight, basis, degree):
    nodes, nfield, levels = fields.shape
    blocks, _, size, _ = operators.shape
    modes = basis.shape[1]
    rads = lax.axis_size("rad")
    fields = fields.reshape(nodes, levels)
    velocity = velocity.reshape(2 * nodes, levels)
    wide = shape((nodes, levels), F32)
    thin = shape((nodes, levels), BF)

    dhat = cheb_matrix(rads * levels)
    dhat = np.stack([dhat[:, c * levels : (c + 1) * levels] for c in range(rads)])
    dh_high = dhat.astype(BF)
    dh_low = (dhat - dh_high.astype(np.float32)).astype(BF)

    half = shape((modes // 2, levels), F32)
    dma = pltpu.SemaphoreType.DMA
    fields, rounded, ids = call(
        round_kernel,
        (wide, thin, shape(neighbours.shape, neighbours.dtype)),
        (fields, neighbours),
        "hh",
        (dma((3,)), dma(())),
    )
    low, high = halo(rounded)
    lap_dense, lap_own = call(
        prepare_kernel,
        (shape((1, 3 * blocks, nodes, size), BF), wide),
        (ids, operators, rounded),
        "shv",
        (dma(neighbours.shape),),
    )
    lap = call(first_lap_kernel, thin, (lap_dense, lap_own, low, high))
    low_two, high_two = halo(lap)
    part = call(
        advect_kernel,
        wide,
        (ids, operators, velocity, lap_dense, low, rounded, high, lap, fields),
        "shhvvvvvv",
        (
            pltpu.VMEM((2, 3 * blocks, nodes, size), BF),
            pltpu.VMEM((2 * nodes, levels), F32),
            dma(()),
            dma(neighbours.shape),
        ),
    )
    stepped, narrow = call(second_lap_kernel, (wide, thin), (lap_dense, low_two, high_two, part))
    shards = [narrow] + [lax.ppermute(narrow, "rad", shift("rad", d)) for d in range(1, rads)]
    wbt, early, bg_high, bg_low = call(
        project_kernel,
        (shape((modes, nodes), BF), shape((modes, levels), F32)) + (shape((2, nodes, modes // 2), BF),) * 2,
        (basis, quad_weight[None, :], degree[None, :], stepped),
        "hhhv",
        (pltpu.VMEM((nodes, modes), F32), pltpu.VMEM((1, nodes), F32), pltpu.VMEM((1, modes), jnp.int32), dma((3,))),
    )
    diffused, keep, send = call(
        lambda *refs: diffuse_kernel(rads, *refs),
        (wide, half, half),
        (*shards, stepped, jnp.asarray(dh_high), jnp.asarray(dh_low), kappa_ref.reshape(rads, 1, levels))
        + (wbt, early),
    )
    mine = chip_sum(keep + swap(send))
    other = swap(mine)
    some = call(lambda *refs: filter_kernel(0, *refs), wide, (diffused, mine, bg_high, bg_low))
    filtered = call(lambda *refs: filter_kernel(1, *refs), wide, (some, other, bg_high, bg_low))
    return filtered.reshape(nodes, nfield, levels)


def solution(mesh):
    return jax.shard_map(
        body,
        mesh=mesh,
        in_specs=(
            P("tile", None, "rad"),
            P("tile", None, "rad"),
            P("tile", None, None, None),
            P("tile", None),
            P(),
            P("tile"),
            P("tile", None),
            P(),
        ),
        out_specs=P("tile", None, "rad"),
        check_vma=False,
    )
```

```python
import math

import jax
import jax.numpy as jnp
import numpy as np
from jax import lax
from jax.experimental import pallas as pl
from jax.experimental.pallas import tpu as pltpu
from jax.sharding import PartitionSpec as P

DEGMAX = 22

advect_step = 0.25
hyper_rate = 0.1
radial_step = 0.25

BF = jnp.bfloat16
F32 = jnp.float32
VMEM = pl.BlockSpec(memory_space=pltpu.VMEM)
SMEM = pl.BlockSpec(memory_space=pltpu.SMEM)
HBM = pl.BlockSpec(memory_space=pltpu.HBM)
PARAMS = pltpu.CompilerParams(vmem_limit_bytes=32 * 1024 * 1024)


def cheb_matrix(count):
    points = np.arange(count)
    angles = np.pi * points / (count - 1)
    upper, lower = angles[:, None], angles[None, :]
    spacing = -2.0 * np.sin((upper + lower) / 2.0) * np.sin((upper - lower) / 2.0)
    np.fill_diagonal(spacing, 1.0)
    weights = np.where((points == 0) | (points == count - 1), 2.0, 1.0)
    parity = np.where((upper * 0 + points[:, None] + points[None, :]) % 2 == 0, 1.0, -1.0)
    entries = weights[:, None] / weights[None, :] * parity / spacing
    np.fill_diagonal(entries, 0.0)
    matrix = entries - np.diag(entries.sum(axis=1))
    return (np.sin(angles)[:, None] * matrix / count).T.astype(np.float32)


def split(value):
    high = value.astype(BF)
    return high, (value - high.astype(F32)).astype(BF)


def dot(left, right):
    return jnp.dot(left, right, preferred_element_type=F32)


def dot3(left, right):
    wide = dot(left[0], jnp.concatenate(right, axis=1))
    count = right[0].shape[1]
    return wide[:, :count] + (wide[:, count:] + dot(left[1], right[0]))


def call(kernel, outs, args, spaces=None, scratch=()):
    spaces = spaces or "v" * len(args)
    args = [pltpu.with_memory_space_constraint(a, pltpu.HBM) if c == "h" else a for a, c in zip(args, spaces)]
    return pl.pallas_call(
        kernel,
        out_shape=outs,
        in_specs=[{"s": SMEM, "h": HBM, "v": VMEM}[c] for c in spaces],
        out_specs=jax.tree.map(lambda _: VMEM, outs),
        scratch_shapes=list(scratch),
        compiler_params=PARAMS,
    )(*args)


def shape(dims, kind):
    return jax.ShapeDtypeStruct(dims, kind)


def beside(dense, first, count):
    return jnp.concatenate([dense[first + s] for s in range(count)], axis=1)


def local_id(ids, b, k, blocks):
    total = blocks * lax.axis_size("tile")
    return lax.rem(ids[b, k] - (lax.axis_index("tile") - 1) * blocks + total, total)


def round_kernel(fields, neighbours, wide, narrow, ids, sems, ids_sem):
    parts = sems.shape[0]
    rows = wide.shape[0] // parts
    copies = []
    for p in range(parts):
        piece = pl.ds(p * rows, rows)
        copies.append(pltpu.make_async_copy(fields.at[piece], wide.at[piece], sems.at[p]))
        copies[-1].start()
    ids_copy = pltpu.make_async_copy(neighbours, ids, ids_sem)
    ids_copy.start()
    for p in range(parts):
        copies[p].wait()
        piece = slice(p * rows, (p + 1) * rows)
        narrow[piece] = wide[piece].astype(BF)
    ids_copy.wait()


def prepare_kernel(ids, ops, own, dense, lap_own, held, sems):
    blocks, _, size, wide = ops.shape
    copies = [pltpu.make_async_copy(ops.at[b, 2], held.at[b], sems.at[b]) for b in range(blocks)]
    for copy in copies:
        copy.start()
    dense[...] = jnp.zeros(dense.shape, BF)
    for b in range(blocks):
        copies[b].wait()
        for k in range(wide // size):
            dense[local_id(ids, b, k, blocks), b * size : (b + 1) * size, :] = held[b, :, k * size : (k + 1) * size]
    lap_own[...] = dot(beside(dense, blocks, blocks), own[...])


def around(dense, low, high):
    blocks = dense.shape[0] // 3
    return dot(beside(dense, 0, blocks), low[...]) + dot(beside(dense, 2 * blocks, blocks), high[...])


def first_lap_kernel(dense, lap_own, low, high, lap):
    lap[...] = (lap_own[...] + around(dense, low, high)).astype(BF)


def advect_kernel(ids, ops, velocity, lap_dense, low, own, high, lap, fields, out, window):
    blocks, _, size, wide = ops.shape
    nodes = own.shape[0]
    for k, tile in enumerate((low, own, high)):
        window[k * nodes : (k + 1) * nodes] = tile[...]
    lap_two = dot(beside(lap_dense, blocks, blocks), lap[...])
    for b in range(blocks):
        starts = [pl.multiple_of(local_id(ids, b, k, blocks) * size, size) for k in range(wide // size)]
        nearby = jnp.concatenate([window[pl.ds(start, size), :] for start in starts], axis=0)
        grad = dot(ops[b, 0:2].reshape(2 * size, wide), nearby)
        vel_x = velocity[pl.ds(2 * b * size, size, stride=2), :]
        vel_y = velocity[pl.ds(2 * b * size + 1, size, stride=2), :]
        rows = slice(b * size, (b + 1) * size)
        value = fields[rows] - advect_step * (vel_x * grad[:size] + vel_y * grad[size:])
        out[rows] = value - hyper_rate * lap_two[rows]


def second_lap_kernel(dense, low, high, part, stepped, narrow):
    value = part[...] - hyper_rate * around(dense, low, high)
    stepped[...] = value
    narrow[...] = value.astype(BF)


def project_kernel(basis, weight, degree, value, wbt, early, bg_high, bg_low, held, weight_held, degree_held, sems):
    nodes, modes = held.shape
    pairs = ((basis, held), (weight, weight_held), (degree, degree_held))
    copies = [pltpu.make_async_copy(*pair, sems.at[k]) for k, pair in enumerate(pairs)]
    for copy in copies:
        copy.start()
    for copy in copies:
        copy.wait()
    parts = split(held[...].T * weight_held[...])
    wbt[...] = parts[0]
    early[...] = dot3(parts, split(value[...]))
    ratio = degree_held[...].astype(F32) / DEGMAX
    gain = 0.5 * math.sqrt(modes / (nodes * lax.axis_size("tile"))) * (1.0 - jnp.exp(-4.0 * ratio * ratio))
    half = modes // 2
    for c in range(2):
        cols = slice(c * half, (c + 1) * half)
        bg_high[c], bg_low[c] = split(held[:, cols] * gain[:, cols])


def diffuse_kernel(count, *refs):
    shards = refs[:count]
    stepped, dh_high, dh_low, kappa, wbt, early, diffused, keep, send = refs[count:]
    rad, core = lax.axis_index("rad"), lax.rem(lax.axis_index("tile"), 2)
    width = stepped.shape[1]
    chunk = [lax.rem(rad + count - d, count) for d in range(count)]
    rows = [pl.ds(pl.multiple_of(c * width, width), width) for c in chunk]
    value = jnp.concatenate([shard[...] for shard in shards], axis=1)
    term = None
    group = 2 if count % 2 == 0 else 1
    for first in range(0, count, group):
        some = range(first, first + group)
        slopes = None
        for table in (dh_high, dh_low):
            weights = [jnp.concatenate([table[chunk[i], rows[j], :] for j in range(count)], axis=0) for i in some]
            more = dot(value, jnp.concatenate(weights, axis=1))
            slopes = more if slopes is None else slopes + more
        rate = jnp.concatenate([kappa[chunk[i]] for i in some], axis=1)
        bend = jnp.tanh(value[:, first * width : (first + group) * width].astype(F32))
        fluxes = (rate + (0.5 * rate) * bend) * slopes
        own = [jnp.concatenate([table[rad, rows[i], :] for i in some], axis=0) for table in (dh_high, dh_low)]
        more = dot3(split(fluxes), own)
        term = more if term is None else term + more
    term = radial_step * term
    diffused[...] = stepped[...] + term
    late = jnp.concatenate(split(term), axis=1)
    half = keep.shape[0]
    for out, which in ((send, 1 - core), (keep, core)):
        modes = pl.ds(pl.multiple_of(which * half, half), half)
        total = dot(wbt[modes, :], late)
        out[...] = early[modes, :] + total[:, :width] + total[:, width:]


def pack_kernel(keep, received, out, scaled):
    value = keep[...] + received[...]
    out[...] = value
    top = jnp.max(jnp.abs(value), axis=(0, 1), keepdims=True)
    power = jnp.round(jnp.log2(jnp.maximum(top, 1e-30)))
    rows = value.shape[0]
    scaled[0:rows] = value * jnp.exp2(8.0 - power)
    scaled[rows:] = jnp.broadcast_to(power, (16, value.shape[1]))


def filter_kernel(swap, value, modes, bg_high, bg_low, out):
    which = lax.rem(lax.axis_index("tile") + swap, 2)
    out[...] = value[...] - dot3((bg_high[which], bg_low[which]), split(modes[...]))


def shift(axis, by):
    count = lax.axis_size(axis)
    return [(i, (i + by) % count) for i in range(count)]


def halo(block):
    high = lax.ppermute(block, "tile", shift("tile", -1))
    low = lax.ppermute(block, "tile", shift("tile", 1))
    return low, high


def swap(block):
    return lax.ppermute(block, "tile", [(i, i ^ 1) for i in range(lax.axis_size("tile"))])


def unpacked(sent):
    rows = sent.shape[0] - 16
    return sent[:rows].astype(F32) * jnp.exp2(sent[rows : rows + 1].astype(F32) - 8.0)


def tile_sum(keep, send):
    count = lax.axis_size("tile")
    received = swap(send)
    if count <= 8:
        rows, levels = keep.shape
        block, scaled = call(pack_kernel, (shape(keep.shape, F32), shape((rows + 16, levels), F32)), (keep, received))
        sent = scaled.astype(jnp.float16)
        parts = [lax.ppermute(sent, "tile", [(i, i ^ m) for i in range(count)]) for m in reversed(range(2, count, 2))]
        return sum((unpacked(part) for part in parts), block)
    block = keep + received
    for m in [1 << k for k in range(1, count.bit_length() - 1)]:
        block = block + lax.ppermute(block, "tile", [(i, i ^ m) for i in range(count)])
    return block


def body(fields, velocity, operators, neighbours, kappa_ref, quad_weight, basis, degree):
    nodes, nfield, levels = fields.shape
    blocks, _, size, _ = operators.shape
    modes = basis.shape[1]
    rads = lax.axis_size("rad")
    fields = fields.reshape(nodes, levels)
    velocity = velocity.reshape(2 * nodes, levels)
    wide = shape((nodes, levels), F32)
    thin = shape((nodes, levels), BF)

    dhat = cheb_matrix(rads * levels)
    dhat = np.stack([dhat[:, c * levels : (c + 1) * levels] for c in range(rads)])
    dh_high = dhat.astype(BF)
    dh_low = (dhat - dh_high.astype(np.float32)).astype(BF)

    half = shape((modes // 2, levels), F32)
    dma = pltpu.SemaphoreType.DMA
    fields, rounded, ids = call(
        round_kernel,
        (wide, thin, shape(neighbours.shape, neighbours.dtype)),
        (fields, neighbours),
        "hh",
        (dma((3,)), dma(())),
    )
    low, high = halo(rounded)
    lap_dense, lap_own = call(
        prepare_kernel,
        (shape((3 * blocks, nodes, size), BF), wide),
        (ids, operators, rounded),
        "shv",
        (pltpu.VMEM((blocks, size, operators.shape[3]), BF), dma((blocks,))),
    )
    lap = call(first_lap_kernel, thin, (lap_dense, lap_own, low, high))
    low_two, high_two = halo(lap)
    part = call(
        advect_kernel,
        wide,
        (ids, operators, velocity, lap_dense, low, rounded, high, lap, fields),
        "svvvvvvvv",
        (pltpu.VMEM((3 * nodes, levels), BF),),
    )
    stepped, narrow = call(second_lap_kernel, (wide, thin), (lap_dense, low_two, high_two, part))
    shards = [narrow] + [lax.ppermute(narrow, "rad", shift("rad", d)) for d in range(1, rads)]
    wbt, early, bg_high, bg_low = call(
        project_kernel,
        (shape((modes, nodes), BF), shape((modes, levels), F32)) + (shape((2, nodes, modes // 2), BF),) * 2,
        (basis, quad_weight[None, :], degree[None, :], stepped),
        "hhhv",
        (pltpu.VMEM((nodes, modes), F32), pltpu.VMEM((1, nodes), F32), pltpu.VMEM((1, modes), jnp.int32), dma((3,))),
    )
    diffused, keep, send = call(
        lambda *refs: diffuse_kernel(rads, *refs),
        (wide, half, half),
        (*shards, stepped, jnp.asarray(dh_high), jnp.asarray(dh_low), kappa_ref.reshape(rads, 1, levels))
        + (wbt, early),
    )
    mine = tile_sum(keep, send)
    other = swap(mine)
    some = call(lambda *refs: filter_kernel(0, *refs), wide, (diffused, mine, bg_high, bg_low))
    filtered = call(lambda *refs: filter_kernel(1, *refs), wide, (some, other, bg_high, bg_low))
    return filtered.reshape(nodes, nfield, levels)


def solution(mesh):
    return jax.shard_map(
        body,
        mesh=mesh,
        in_specs=(
            P("tile", None, "rad"),
            P("tile", None, "rad"),
            P("tile", None, None, None),
            P("tile", None),
            P(),
            P("tile"),
            P("tile", None),
            P(),
        ),
        out_specs=P("tile", None, "rad"),
        check_vma=False,
    )
```

```python
import math

import jax
import jax.numpy as jnp
import numpy as np
from jax import lax
from jax.experimental import pallas as pl
from jax.experimental.pallas import tpu as pltpu
from jax.sharding import PartitionSpec as P

DEGMAX = 22

advect_step = 0.25
hyper_rate = 0.1
radial_step = 0.25

BF = jnp.bfloat16
F32 = jnp.float32
VMEM = pl.BlockSpec(memory_space=pltpu.VMEM)
SMEM = pl.BlockSpec(memory_space=pltpu.SMEM)
HBM = pl.BlockSpec(memory_space=pltpu.HBM)
PARAMS = pltpu.CompilerParams(vmem_limit_bytes=32 * 1024 * 1024)


def cheb_matrix(count):
    points = np.arange(count)
    angles = np.pi * points / (count - 1)
    upper, lower = angles[:, None], angles[None, :]
    spacing = -2.0 * np.sin((upper + lower) / 2.0) * np.sin((upper - lower) / 2.0)
    np.fill_diagonal(spacing, 1.0)
    weights = np.where((points == 0) | (points == count - 1), 2.0, 1.0)
    parity = np.where((upper * 0 + points[:, None] + points[None, :]) % 2 == 0, 1.0, -1.0)
    entries = weights[:, None] / weights[None, :] * parity / spacing
    np.fill_diagonal(entries, 0.0)
    matrix = entries - np.diag(entries.sum(axis=1))
    return (np.sin(angles)[:, None] * matrix / count).T.astype(np.float32)


def split(value):
    high = value.astype(BF)
    return high, (value - high.astype(F32)).astype(BF)


def dot(left, right):
    return jnp.dot(left, right, preferred_element_type=F32)


def dot3(left, right):
    wide = dot(left[0], jnp.concatenate(right, axis=1))
    count = right[0].shape[1]
    return wide[:, :count] + (wide[:, count:] + dot(left[1], right[0]))


def call(kernel, outs, args, spaces=None, scratch=()):
    spaces = spaces or "v" * len(args)
    args = [pltpu.with_memory_space_constraint(a, pltpu.HBM) if c == "h" else a for a, c in zip(args, spaces)]
    return pl.pallas_call(
        kernel,
        out_shape=outs,
        in_specs=[{"s": SMEM, "h": HBM, "v": VMEM}[c] for c in spaces],
        out_specs=jax.tree.map(lambda _: VMEM, outs),
        scratch_shapes=list(scratch),
        compiler_params=PARAMS,
    )(*args)


def shape(dims, kind):
    return jax.ShapeDtypeStruct(dims, kind)


def beside(dense, first, count):
    return jnp.concatenate([dense[first + s] for s in range(count)], axis=1)


def local_id(ids, b, k, blocks):
    total = blocks * lax.axis_size("tile")
    return lax.rem(ids[b, k] - (lax.axis_index("tile") - 1) * blocks + total, total)


def round_kernel(fields, neighbours, wide, narrow, ids, sems, ids_sem):
    parts = sems.shape[0]
    rows = wide.shape[0] // parts
    copies = []
    for p in range(parts):
        piece = pl.ds(p * rows, rows)
        copies.append(pltpu.make_async_copy(fields.at[piece], wide.at[piece], sems.at[p]))
        copies[-1].start()
    ids_copy = pltpu.make_async_copy(neighbours, ids, ids_sem)
    ids_copy.start()
    for p in range(parts):
        copies[p].wait()
        piece = slice(p * rows, (p + 1) * rows)
        narrow[piece] = wide[piece].astype(BF)
    ids_copy.wait()


def prepare_kernel(ids, ops, own, dense, lap_own, held, sems):
    blocks, _, size, wide = ops.shape
    copies = [pltpu.make_async_copy(ops.at[b, 2], held.at[b], sems.at[b]) for b in range(blocks)]
    for copy in copies:
        copy.start()
    dense[...] = jnp.zeros(dense.shape, BF)
    for b in range(blocks):
        copies[b].wait()
        for k in range(wide // size):
            dense[local_id(ids, b, k, blocks), b * size : (b + 1) * size, :] = held[b, :, k * size : (k + 1) * size]
    lap_own[...] = dot(beside(dense, blocks, blocks), own[...])


def around(dense, low, high):
    blocks = dense.shape[0] // 3
    return dot(beside(dense, 0, blocks), low[...]) + dot(beside(dense, 2 * blocks, blocks), high[...])


def first_lap_kernel(dense, lap_own, high, low, lap):
    lap[...] = (lap_own[...] + around(dense, low, high)).astype(BF)


def advect_kernel(ids, ops, velocity, lap_dense, low, own, high, lap, fields, out, window):
    blocks, _, size, wide = ops.shape
    nodes = own.shape[0]
    for k, tile in enumerate((low, own, high)):
        window[k * nodes : (k + 1) * nodes] = tile[...]
    lap_two = dot(beside(lap_dense, blocks, blocks), lap[...])
    for b in range(blocks):
        starts = [pl.multiple_of(local_id(ids, b, k, blocks) * size, size) for k in range(wide // size)]
        nearby = jnp.concatenate([window[pl.ds(start, size), :] for start in starts], axis=0)
        grad = dot(ops[b, 0:2].reshape(2 * size, wide), nearby)
        vel_x = velocity[pl.ds(2 * b * size, size, stride=2), :]
        vel_y = velocity[pl.ds(2 * b * size + 1, size, stride=2), :]
        rows = slice(b * size, (b + 1) * size)
        value = fields[rows] - advect_step * (vel_x * grad[:size] + vel_y * grad[size:])
        out[rows] = value - hyper_rate * lap_two[rows]


def second_lap_kernel(dense, high, low, part, stepped, narrow):
    value = part[...] - hyper_rate * around(dense, low, high)
    stepped[...] = value
    narrow[...] = value.astype(BF)


def project_kernel(basis, weight, degree, value, wbt, early, bg_high, bg_low, held, weight_held, degree_held, sems):
    nodes, modes = held.shape
    pairs = ((basis, held), (weight, weight_held), (degree, degree_held))
    copies = [pltpu.make_async_copy(*pair, sems.at[k]) for k, pair in enumerate(pairs)]
    for copy in copies:
        copy.start()
    for copy in copies:
        copy.wait()
    parts = split(held[...].T * weight_held[...])
    wbt[...] = parts[0]
    early[...] = dot3(parts, split(value[...]))
    ratio = degree_held[...].astype(F32) / DEGMAX
    gain = 0.5 * math.sqrt(modes / (nodes * lax.axis_size("tile"))) * (1.0 - jnp.exp(-4.0 * ratio * ratio))
    half = modes // 2
    for c in range(2):
        cols = slice(c * half, (c + 1) * half)
        bg_high[c], bg_low[c] = split(held[:, cols] * gain[:, cols])


def diffuse_kernel(count, *refs):
    shards = refs[:count]
    stepped, dh_high, dh_low, kappa, wbt, early, diffused, keep, send = refs[count:]
    rad, core = lax.axis_index("rad"), lax.rem(lax.axis_index("tile"), 2)
    width = stepped.shape[1]
    chunk = [lax.rem(rad + count - d, count) for d in range(count)]
    rows = [pl.ds(pl.multiple_of(c * width, width), width) for c in chunk]
    value = jnp.concatenate([shard[...] for shard in shards], axis=1)
    term = None
    group = 2 if count % 2 == 0 else 1
    for first in range(0, count, group):
        some = range(first, first + group)
        slopes = None
        for table in (dh_high, dh_low):
            weights = [jnp.concatenate([table[chunk[i], rows[j], :] for j in range(count)], axis=0) for i in some]
            more = dot(value, jnp.concatenate(weights, axis=1))
            slopes = more if slopes is None else slopes + more
        rate = jnp.concatenate([kappa[chunk[i]] for i in some], axis=1)
        bend = jnp.tanh(value[:, first * width : (first + group) * width].astype(F32))
        fluxes = (rate + (0.5 * rate) * bend) * slopes
        own = [jnp.concatenate([table[rad, rows[i], :] for i in some], axis=0) for table in (dh_high, dh_low)]
        more = dot3(split(fluxes), own)
        term = more if term is None else term + more
    term = radial_step * term
    diffused[...] = stepped[...] + term
    late = jnp.concatenate(split(term), axis=1)
    half = keep.shape[0]
    for out, which in ((send, 1 - core), (keep, core)):
        modes = pl.ds(pl.multiple_of(which * half, half), half)
        total = dot(wbt[modes, :], late)
        out[...] = early[modes, :] + total[:, :width] + total[:, width:]


def pack_kernel(keep, received, out, scaled):
    value = keep[...] + received[...]
    out[...] = value
    top = jnp.max(jnp.abs(value), axis=(0, 1), keepdims=True)
    power = jnp.round(jnp.log2(jnp.maximum(top, 1e-30)))
    rows = value.shape[0]
    scaled[0:rows] = value * jnp.exp2(8.0 - power)
    scaled[rows:] = jnp.broadcast_to(power, (16, value.shape[1]))


def filter_kernel(swap, value, modes, bg_high, bg_low, out):
    which = lax.rem(lax.axis_index("tile") + swap, 2)
    out[...] = value[...] - dot3((bg_high[which], bg_low[which]), split(modes[...]))


def shift(axis, by):
    count = lax.axis_size(axis)
    return [(i, (i + by) % count) for i in range(count)]


def halo(block):
    high = lax.ppermute(block, "tile", shift("tile", -1))
    low = lax.ppermute(block, "tile", shift("tile", 1))
    return low, high


def swap(block):
    return lax.ppermute(block, "tile", [(i, i ^ 1) for i in range(lax.axis_size("tile"))])


def unpacked(sent):
    rows = sent.shape[0] - 16
    return sent[:rows].astype(F32) * jnp.exp2(sent[rows : rows + 1].astype(F32) - 8.0)


def tile_sum(keep, send):
    count = lax.axis_size("tile")
    received = swap(send)
    if count <= 8:
        rows, levels = keep.shape
        block, scaled = call(pack_kernel, (shape(keep.shape, F32), shape((rows + 16, levels), F32)), (keep, received))
        sent = scaled.astype(jnp.float16)
        parts = [lax.ppermute(sent, "tile", [(i, i ^ m) for i in range(count)]) for m in reversed(range(2, count, 2))]
        return sum((unpacked(part) for part in parts), block)
    block = keep + received
    for m in [1 << k for k in range(1, count.bit_length() - 1)]:
        block = block + lax.ppermute(block, "tile", [(i, i ^ m) for i in range(count)])
    return block


def body(fields, velocity, operators, neighbours, kappa_ref, quad_weight, basis, degree):
    nodes, nfield, levels = fields.shape
    blocks, _, size, _ = operators.shape
    modes = basis.shape[1]
    rads = lax.axis_size("rad")
    fields = fields.reshape(nodes, levels)
    velocity = velocity.reshape(2 * nodes, levels)
    wide = shape((nodes, levels), F32)
    thin = shape((nodes, levels), BF)

    dhat = cheb_matrix(rads * levels)
    dhat = np.stack([dhat[:, c * levels : (c + 1) * levels] for c in range(rads)])
    dh_high = dhat.astype(BF)
    dh_low = (dhat - dh_high.astype(np.float32)).astype(BF)

    half = shape((modes // 2, levels), F32)
    dma = pltpu.SemaphoreType.DMA
    fields, rounded, ids = call(
        round_kernel,
        (wide, thin, shape(neighbours.shape, neighbours.dtype)),
        (fields, neighbours),
        "hh",
        (dma((3,)), dma(())),
    )
    low, high = halo(rounded)
    lap_dense, lap_own = call(
        prepare_kernel,
        (shape((3 * blocks, nodes, size), BF), wide),
        (ids, operators, rounded),
        "shv",
        (pltpu.VMEM((blocks, size, operators.shape[3]), BF), dma((blocks,))),
    )
    lap = call(first_lap_kernel, thin, (lap_dense, lap_own, high, low))
    low_two, high_two = halo(lap)
    part = call(
        advect_kernel,
        wide,
        (ids, operators, velocity, lap_dense, low, rounded, high, lap, fields),
        "svvvvvvvv",
        (pltpu.VMEM((3 * nodes, levels), BF),),
    )
    stepped, narrow = call(second_lap_kernel, (wide, thin), (lap_dense, high_two, low_two, part))
    shards = [narrow] + [lax.ppermute(narrow, "rad", shift("rad", d)) for d in range(1, rads)]
    wbt, early, bg_high, bg_low = call(
        project_kernel,
        (shape((modes, nodes), BF), shape((modes, levels), F32)) + (shape((2, nodes, modes // 2), BF),) * 2,
        (basis, quad_weight[None, :], degree[None, :], stepped),
        "hhhv",
        (pltpu.VMEM((nodes, modes), F32), pltpu.VMEM((1, nodes), F32), pltpu.VMEM((1, modes), jnp.int32), dma((3,))),
    )
    diffused, keep, send = call(
        lambda *refs: diffuse_kernel(rads, *refs),
        (wide, half, half),
        (*shards, stepped, jnp.asarray(dh_high), jnp.asarray(dh_low), kappa_ref.reshape(rads, 1, levels))
        + (wbt, early),
    )
    mine = tile_sum(keep, send)
    other = swap(mine)
    some = call(lambda *refs: filter_kernel(0, *refs), wide, (diffused, mine, bg_high, bg_low))
    filtered = call(lambda *refs: filter_kernel(1, *refs), wide, (some, other, bg_high, bg_low))
    return filtered.reshape(nodes, nfield, levels)


def solution(mesh):
    return jax.shard_map(
        body,
        mesh=mesh,
        in_specs=(
            P("tile", None, "rad"),
            P("tile", None, "rad"),
            P("tile", None, None, None),
            P("tile", None),
            P(),
            P("tile"),
            P("tile", None),
            P(),
        ),
        out_specs=P("tile", None, "rad"),
        check_vma=False,
    )
```

```python
import math

import jax
import jax.numpy as jnp
import numpy as np
from jax import lax
from jax.experimental import pallas as pl
from jax.experimental.pallas import tpu as pltpu
from jax.sharding import PartitionSpec as P

DEGMAX = 22

advect_step = 0.25
hyper_rate = 0.1
radial_step = 0.25

BF = jnp.bfloat16
F32 = jnp.float32
VMEM = pl.BlockSpec(memory_space=pltpu.VMEM)
SMEM = pl.BlockSpec(memory_space=pltpu.SMEM)
HBM = pl.BlockSpec(memory_space=pltpu.HBM)
PARAMS = pltpu.CompilerParams(vmem_limit_bytes=32 * 1024 * 1024)


def cheb_matrix(count):
    points = np.arange(count)
    angles = np.pi * points / (count - 1)
    upper, lower = angles[:, None], angles[None, :]
    spacing = -2.0 * np.sin((upper + lower) / 2.0) * np.sin((upper - lower) / 2.0)
    np.fill_diagonal(spacing, 1.0)
    weights = np.where((points == 0) | (points == count - 1), 2.0, 1.0)
    parity = np.where((upper * 0 + points[:, None] + points[None, :]) % 2 == 0, 1.0, -1.0)
    entries = weights[:, None] / weights[None, :] * parity / spacing
    np.fill_diagonal(entries, 0.0)
    matrix = entries - np.diag(entries.sum(axis=1))
    return (np.sin(angles)[:, None] * matrix / count).T.astype(np.float32)


def split(value):
    high = value.astype(BF)
    return high, (value - high.astype(F32)).astype(BF)


def dot(left, right):
    return jnp.dot(left, right, preferred_element_type=F32)


def dot3(left, right):
    wide = dot(left[0], jnp.concatenate(right, axis=1))
    count = right[0].shape[1]
    return wide[:, :count] + (wide[:, count:] + dot(left[1], right[0]))


def call(kernel, outs, args, spaces=None, scratch=()):
    spaces = spaces or "v" * len(args)
    args = [pltpu.with_memory_space_constraint(a, pltpu.HBM) if c == "h" else a for a, c in zip(args, spaces)]
    return pl.pallas_call(
        kernel,
        out_shape=outs,
        in_specs=[{"s": SMEM, "h": HBM, "v": VMEM}[c] for c in spaces],
        out_specs=jax.tree.map(lambda _: VMEM, outs),
        scratch_shapes=list(scratch),
        compiler_params=PARAMS,
    )(*args)


def shape(dims, kind):
    return jax.ShapeDtypeStruct(dims, kind)


def beside(dense, first, count):
    return jnp.concatenate([dense[first + s] for s in range(count)], axis=1)


def local_id(ids, b, k, blocks):
    total = blocks * lax.axis_size("tile")
    return lax.rem(ids[b, k] - (lax.axis_index("tile") - 1) * blocks + total, total)


def round_kernel(fields, neighbours, wide, narrow, ids, sems, ids_sem):
    parts = sems.shape[0]
    rows = wide.shape[0] // parts
    copies = []
    for p in range(parts):
        piece = pl.ds(p * rows, rows)
        copies.append(pltpu.make_async_copy(fields.at[piece], wide.at[piece], sems.at[p]))
        copies[-1].start()
    ids_copy = pltpu.make_async_copy(neighbours, ids, ids_sem)
    ids_copy.start()
    for p in range(parts):
        copies[p].wait()
        piece = slice(p * rows, (p + 1) * rows)
        narrow[piece] = wide[piece].astype(BF)
    ids_copy.wait()


def prepare_kernel(ids, ops, own, dense, lap_own, held, sems):
    blocks, _, size, wide = ops.shape
    copies = [pltpu.make_async_copy(ops.at[b, 2], held.at[b], sems.at[b]) for b in range(blocks)]
    for copy in copies:
        copy.start()
    dense[...] = jnp.zeros(dense.shape, BF)
    for b in range(blocks):
        copies[b].wait()
        for k in range(wide // size):
            dense[local_id(ids, b, k, blocks), b * size : (b + 1) * size, :] = held[b, :, k * size : (k + 1) * size]
    lap_own[...] = dot(beside(dense, blocks, blocks), own[...])


def around(dense, low, high):
    blocks = dense.shape[0] // 3
    return dot(beside(dense, 0, blocks), low[...]) + dot(beside(dense, 2 * blocks, blocks), high[...])


def first_lap_kernel(dense, lap_own, high, low, lap):
    lap[...] = (lap_own[...] + around(dense, low, high)).astype(BF)


def advect_kernel(ids, ops, velocity, lap_dense, low, own, high, lap, fields, out, window):
    blocks, _, size, wide = ops.shape
    nodes = own.shape[0]
    for k, tile in enumerate((low, own, high)):
        window[k * nodes : (k + 1) * nodes] = tile[...]
    lap_two = dot(beside(lap_dense, blocks, blocks), lap[...])
    for b in range(blocks):
        starts = [pl.multiple_of(local_id(ids, b, k, blocks) * size, size) for k in range(wide // size)]
        nearby = jnp.concatenate([window[pl.ds(start, size), :] for start in starts], axis=0)
        grad = dot(ops[b, 0:2].reshape(2 * size, wide), nearby)
        vel_x = velocity[pl.ds(2 * b * size, size, stride=2), :]
        vel_y = velocity[pl.ds(2 * b * size + 1, size, stride=2), :]
        rows = slice(b * size, (b + 1) * size)
        value = fields[rows] - advect_step * (vel_x * grad[:size] + vel_y * grad[size:])
        out[rows] = value - hyper_rate * lap_two[rows]


def second_lap_kernel(dense, high, low, part, stepped, narrow):
    value = part[...] - hyper_rate * around(dense, low, high)
    stepped[...] = value
    narrow[...] = value.astype(BF)


def project_kernel(basis, weight, degree, value, wbt, early, bg_high, bg_low, held, weight_held, degree_held, sems):
    nodes, modes = held.shape
    pairs = ((basis, held), (weight, weight_held), (degree, degree_held))
    copies = [pltpu.make_async_copy(*pair, sems.at[k]) for k, pair in enumerate(pairs)]
    for copy in copies:
        copy.start()
    for copy in copies:
        copy.wait()
    parts = split(held[...].T * weight_held[...])
    wbt[...] = parts[0]
    early[...] = dot3(parts, split(value[...]))
    ratio = degree_held[...].astype(F32) / DEGMAX
    gain = 0.5 * math.sqrt(modes / (nodes * lax.axis_size("tile"))) * (1.0 - jnp.exp(-4.0 * ratio * ratio))
    half = modes // 2
    for c in range(2):
        cols = slice(c * half, (c + 1) * half)
        bg_high[c], bg_low[c] = split(held[:, cols] * gain[:, cols])


def source(rad, d):
    count = lax.axis_size("rad")
    return (rad + count - d) % count if isinstance(rad, int) else lax.rem(rad + count - d, count)


def diffuse_kernel(order, *refs):
    count = len(order)
    shards = refs[:count]
    stepped, dh_high, dh_low, kappa, wbt, early, diffused, keep, send = refs[count:]
    rad, core = lax.axis_index("rad"), lax.rem(lax.axis_index("tile"), 2)
    width = stepped.shape[1]
    chunk = [source(rad, d) for d in order]
    rows = [pl.ds(pl.multiple_of(c * width, width), width) for c in chunk]
    value = jnp.concatenate([shard[...] for shard in shards], axis=1)
    slopes = None
    for table in (dh_high, dh_low):
        weights = [jnp.concatenate([table[c, r, :] for r in rows], axis=0) for c in chunk]
        more = dot(value, jnp.concatenate(weights, axis=1))
        slopes = more if slopes is None else slopes + more
    rate = jnp.concatenate([kappa[c] for c in chunk], axis=1)
    fluxes = (rate + (0.5 * rate) * jnp.tanh(value.astype(F32))) * slopes
    own = [jnp.concatenate([table[rad, r, :] for r in rows], axis=0) for table in (dh_high, dh_low)]
    term = dot3(split(fluxes), own)
    term = radial_step * term
    diffused[...] = stepped[...] + term
    late = jnp.concatenate(split(term), axis=1)
    half = keep.shape[0]
    for out, which in ((send, 1 - core), (keep, core)):
        modes = pl.ds(pl.multiple_of(which * half, half), half)
        total = dot(wbt[modes, :], late)
        out[...] = early[modes, :] + total[:, :width] + total[:, width:]


def pack_kernel(keep, received, out, scaled):
    value = keep[...] + received[...]
    out[...] = value
    top = jnp.max(jnp.abs(value), axis=(0, 1), keepdims=True)
    power = jnp.round(jnp.log2(jnp.maximum(top, 1e-30)))
    rows = value.shape[0]
    scaled[0:rows] = value * jnp.exp2(8.0 - power)
    scaled[rows:] = jnp.broadcast_to(power, (16, value.shape[1]))


def filter_kernel(swap, value, modes, bg_high, bg_low, out):
    which = lax.rem(lax.axis_index("tile") + swap, 2)
    out[...] = value[...] - dot3((bg_high[which], bg_low[which]), split(modes[...]))


def shift(axis, by):
    count = lax.axis_size(axis)
    return [(i, (i + by) % count) for i in range(count)]


def halo(block):
    high = lax.ppermute(block, "tile", shift("tile", -1))
    low = lax.ppermute(block, "tile", shift("tile", 1))
    return low, high


def swap(block):
    return lax.ppermute(block, "tile", [(i, i ^ 1) for i in range(lax.axis_size("tile"))])


def unpacked(sent):
    rows = sent.shape[0] - 16
    return sent[:rows].astype(F32) * jnp.exp2(sent[rows : rows + 1].astype(F32) - 8.0)


def tile_sum(keep, send):
    count = lax.axis_size("tile")
    received = swap(send)
    if count <= 8:
        rows, levels = keep.shape
        block, scaled = call(pack_kernel, (shape(keep.shape, F32), shape((rows + 16, levels), F32)), (keep, received))
        sent = scaled.astype(jnp.float16)
        parts = [lax.ppermute(sent, "tile", [(i, i ^ m) for i in range(count)]) for m in reversed(range(2, count, 2))]
        return sum((unpacked(part) for part in parts), block)
    block = keep + received
    for m in [1 << k for k in range(1, count.bit_length() - 1)]:
        block = block + lax.ppermute(block, "tile", [(i, i ^ m) for i in range(count)])
    return block


def body(fields, velocity, operators, neighbours, kappa_ref, quad_weight, basis, degree):
    nodes, nfield, levels = fields.shape
    blocks, _, size, _ = operators.shape
    modes = basis.shape[1]
    rads = lax.axis_size("rad")
    fields = fields.reshape(nodes, levels)
    velocity = velocity.reshape(2 * nodes, levels)
    wide = shape((nodes, levels), F32)
    thin = shape((nodes, levels), BF)

    dhat = cheb_matrix(rads * levels)
    dhat = np.stack([dhat[:, c * levels : (c + 1) * levels] for c in range(rads)])
    dh_high = dhat.astype(BF)
    dh_low = (dhat - dh_high.astype(np.float32)).astype(BF)

    half = shape((modes // 2, levels), F32)
    dma = pltpu.SemaphoreType.DMA
    fields, rounded, ids = call(
        round_kernel,
        (wide, thin, shape(neighbours.shape, neighbours.dtype)),
        (fields, neighbours),
        "hh",
        (dma((3,)), dma(())),
    )
    low, high = halo(rounded)
    lap_dense, lap_own = call(
        prepare_kernel,
        (shape((3 * blocks, nodes, size), BF), wide),
        (ids, operators, rounded),
        "shv",
        (pltpu.VMEM((blocks, size, operators.shape[3]), BF), dma((blocks,))),
    )
    lap = call(first_lap_kernel, thin, (lap_dense, lap_own, high, low))
    low_two, high_two = halo(lap)
    part = call(
        advect_kernel,
        wide,
        (ids, operators, velocity, lap_dense, low, rounded, high, lap, fields),
        "svvvvvvvv",
        (pltpu.VMEM((3 * nodes, levels), BF),),
    )
    stepped, narrow = call(second_lap_kernel, (wide, thin), (lap_dense, high_two, low_two, part))
    order = [0, 1, *reversed(range(2, rads))]
    shards = [narrow] + [lax.ppermute(narrow, "rad", [(source(i, d), i) for i in range(rads)]) for d in order[1:]]
    wbt, early, bg_high, bg_low = call(
        project_kernel,
        (shape((modes, nodes), BF), shape((modes, levels), F32)) + (shape((2, nodes, modes // 2), BF),) * 2,
        (basis, quad_weight[None, :], degree[None, :], stepped),
        "hhhv",
        (pltpu.VMEM((nodes, modes), F32), pltpu.VMEM((1, nodes), F32), pltpu.VMEM((1, modes), jnp.int32), dma((3,))),
    )
    diffused, keep, send = call(
        lambda *refs: diffuse_kernel(order, *refs),
        (wide, half, half),
        (*shards, stepped, jnp.asarray(dh_high), jnp.asarray(dh_low), kappa_ref.reshape(rads, 1, levels))
        + (wbt, early),
    )
    mine = tile_sum(keep, send)
    other = swap(mine)
    some = call(lambda *refs: filter_kernel(0, *refs), wide, (diffused, mine, bg_high, bg_low))
    filtered = call(lambda *refs: filter_kernel(1, *refs), wide, (some, other, bg_high, bg_low))
    return filtered.reshape(nodes, nfield, levels)


def solution(mesh):
    return jax.shard_map(
        body,
        mesh=mesh,
        in_specs=(
            P("tile", None, "rad"),
            P("tile", None, "rad"),
            P("tile", None, None, None),
            P("tile", None),
            P(),
            P("tile"),
            P("tile", None),
            P(),
        ),
        out_specs=P("tile", None, "rad"),
        check_vma=False,
    )
```

```python
import math

import jax
import jax.numpy as jnp
import numpy as np
from jax import lax
from jax.experimental import pallas as pl
from jax.experimental.pallas import tpu as pltpu
from jax.sharding import PartitionSpec as P

DEGMAX = 22

advect_step = 0.25
hyper_rate = 0.1
radial_step = 0.25

BF = jnp.bfloat16
F32 = jnp.float32
VMEM = pl.BlockSpec(memory_space=pltpu.VMEM)
SMEM = pl.BlockSpec(memory_space=pltpu.SMEM)
HBM = pl.BlockSpec(memory_space=pltpu.HBM)
PARAMS = pltpu.CompilerParams(vmem_limit_bytes=32 * 1024 * 1024)


def cheb_matrix(count):
    points = np.arange(count)
    angles = np.pi * points / (count - 1)
    upper, lower = angles[:, None], angles[None, :]
    spacing = -2.0 * np.sin((upper + lower) / 2.0) * np.sin((upper - lower) / 2.0)
    np.fill_diagonal(spacing, 1.0)
    weights = np.where((points == 0) | (points == count - 1), 2.0, 1.0)
    parity = np.where((upper * 0 + points[:, None] + points[None, :]) % 2 == 0, 1.0, -1.0)
    entries = weights[:, None] / weights[None, :] * parity / spacing
    np.fill_diagonal(entries, 0.0)
    matrix = entries - np.diag(entries.sum(axis=1))
    return (np.sin(angles)[:, None] * matrix / count).T.astype(np.float32)


def split(value):
    high = value.astype(BF)
    return high, (value - high.astype(F32)).astype(BF)


def dot(left, right):
    return jnp.dot(left, right, preferred_element_type=F32)


def dot3(left, right):
    wide = dot(left[0], jnp.concatenate(right, axis=1))
    count = right[0].shape[1]
    return wide[:, :count] + (wide[:, count:] + dot(left[1], right[0]))


def call(kernel, outs, args, spaces=None, scratch=()):
    spaces = spaces or "v" * len(args)
    args = [pltpu.with_memory_space_constraint(a, pltpu.HBM) if c == "h" else a for a, c in zip(args, spaces)]
    return pl.pallas_call(
        kernel,
        out_shape=outs,
        in_specs=[{"s": SMEM, "h": HBM, "v": VMEM}[c] for c in spaces],
        out_specs=jax.tree.map(lambda _: VMEM, outs),
        scratch_shapes=list(scratch),
        compiler_params=PARAMS,
    )(*args)


def shape(dims, kind):
    return jax.ShapeDtypeStruct(dims, kind)


def beside(dense, first, count):
    return jnp.concatenate([dense[first + s] for s in range(count)], axis=1)


def local_id(ids, b, k, blocks):
    total = blocks * lax.axis_size("tile")
    return lax.rem(ids[b, k] - (lax.axis_index("tile") - 1) * blocks + total, total)


def round_kernel(fields, neighbours, wide, narrow, ids, sems, ids_sem):
    parts = sems.shape[0]
    rows = wide.shape[0] // parts
    copies = []
    for p in range(parts):
        piece = pl.ds(p * rows, rows)
        copies.append(pltpu.make_async_copy(fields.at[piece], wide.at[piece], sems.at[p]))
        copies[-1].start()
    ids_copy = pltpu.make_async_copy(neighbours, ids, ids_sem)
    ids_copy.start()
    for p in range(parts):
        copies[p].wait()
        piece = slice(p * rows, (p + 1) * rows)
        narrow[piece] = wide[piece].astype(BF)
    ids_copy.wait()


def prepare_kernel(ids, ops, own, dense, lap_own, held, sems):
    blocks, _, size, wide = ops.shape
    copies = [pltpu.make_async_copy(ops.at[b, 2], held.at[b], sems.at[b]) for b in range(blocks)]
    for copy in copies:
        copy.start()
    dense[...] = jnp.zeros(dense.shape, BF)
    for b in range(blocks):
        copies[b].wait()
        for k in range(wide // size):
            dense[local_id(ids, b, k, blocks), b * size : (b + 1) * size, :] = held[b, :, k * size : (k + 1) * size]
    lap_own[...] = dot(beside(dense, blocks, blocks), own[...])


def around(dense, low, high):
    blocks = dense.shape[0] // 3
    return dot(beside(dense, 0, blocks), low[...]) + dot(beside(dense, 2 * blocks, blocks), high[...])


def first_lap_kernel(dense, lap_own, high, low, lap):
    lap[...] = (lap_own[...] + around(dense, low, high)).astype(BF)


def advect_kernel(ids, ops, velocity, lap_dense, low, own, high, lap, fields, out, window):
    blocks, _, size, wide = ops.shape
    nodes = own.shape[0]
    for k, tile in enumerate((low, own, high)):
        window[k * nodes : (k + 1) * nodes] = tile[...]
    lap_two = dot(beside(lap_dense, blocks, blocks), lap[...])
    for b in range(blocks):
        starts = [pl.multiple_of(local_id(ids, b, k, blocks) * size, size) for k in range(wide // size)]
        nearby = jnp.concatenate([window[pl.ds(start, size), :] for start in starts], axis=0)
        grad = dot(ops[b, 0:2].reshape(2 * size, wide), nearby)
        vel_x = velocity[pl.ds(2 * b * size, size, stride=2), :]
        vel_y = velocity[pl.ds(2 * b * size + 1, size, stride=2), :]
        rows = slice(b * size, (b + 1) * size)
        value = fields[rows] - advect_step * (vel_x * grad[:size] + vel_y * grad[size:])
        out[rows] = value - hyper_rate * lap_two[rows]


def second_lap_kernel(dense, high, low, part, stepped, narrow):
    value = part[...] - hyper_rate * around(dense, low, high)
    stepped[...] = value
    narrow[...] = value.astype(BF)


def project_kernel(basis, weight, degree, value, wbt, early, bg_high, bg_low, held, weight_held, degree_held, sems):
    nodes, modes = held.shape
    pairs = ((basis, held), (weight, weight_held), (degree, degree_held))
    copies = [pltpu.make_async_copy(*pair, sems.at[k]) for k, pair in enumerate(pairs)]
    for copy in copies:
        copy.start()
    for copy in copies:
        copy.wait()
    parts = split(held[...].T * weight_held[...])
    wbt[...] = parts[0]
    early[...] = dot3(parts, split(value[...]))
    ratio = degree_held[...].astype(F32) / DEGMAX
    gain = 0.5 * math.sqrt(modes / (nodes * lax.axis_size("tile"))) * (1.0 - jnp.exp(-4.0 * ratio * ratio))
    half = modes // 2
    for c in range(2):
        cols = slice(c * half, (c + 1) * half)
        bg_high[c], bg_low[c] = split(held[:, cols] * gain[:, cols])


def source(rad, d):
    count = lax.axis_size("rad")
    return (rad + count - d) % count if isinstance(rad, int) else lax.rem(rad + count - d, count)


def gathered(order, width):
    rad = lax.axis_index("rad")
    chunk = [source(rad, d) for d in order]
    return rad, chunk, [pl.ds(pl.multiple_of(c * width, width), width) for c in chunk]


def early_diffuse_kernel(order, *refs):
    count = len(order)
    shards = refs[: count - 1]
    dh_high, dh_low, kappa, slopes, rates = refs[count - 1 :]
    width = kappa.shape[2]
    _, chunk, rows = gathered(order, width)
    value = jnp.concatenate([shard[...] for shard in shards], axis=1)
    total = None
    for table in (dh_high, dh_low):
        weights = [jnp.concatenate([table[c, r, :] for r in rows[:-1]], axis=0) for c in chunk]
        more = dot(value, jnp.concatenate(weights, axis=1))
        total = more if total is None else total + more
    slopes[...] = total
    rate = jnp.concatenate([kappa[c] for c in chunk[:-1]], axis=1)
    rates[...] = rate + (0.5 * rate) * jnp.tanh(value.astype(F32))


def diffuse_kernel(order, last, stepped, dh_high, dh_low, kappa, wbt, early, slopes, rates, diffused, keep, send):
    width = stepped.shape[1]
    rad, chunk, rows = gathered(order, width)
    core = lax.rem(lax.axis_index("tile"), 2)
    value = last[...]
    weights = [jnp.concatenate([dh_high[c, rows[-1], :], dh_low[c, rows[-1], :]], axis=0) for c in chunk]
    total = slopes[...] + dot(jnp.concatenate([value, value], axis=1), jnp.concatenate(weights, axis=1))
    rate = kappa[chunk[-1]]
    last_rates = rate + (0.5 * rate) * jnp.tanh(value.astype(F32))
    fluxes = jnp.concatenate([rates[...], last_rates], axis=1) * total
    own = [jnp.concatenate([table[rad, r, :] for r in rows], axis=0) for table in (dh_high, dh_low)]
    term = radial_step * dot3(split(fluxes), own)
    diffused[...] = stepped[...] + term
    late = jnp.concatenate(split(term), axis=1)
    half = keep.shape[0]
    for out, which in ((send, 1 - core), (keep, core)):
        modes = pl.ds(pl.multiple_of(which * half, half), half)
        total = dot(wbt[modes, :], late)
        out[...] = early[modes, :] + total[:, :width] + total[:, width:]


def pack_kernel(keep, received, out, scaled):
    value = keep[...] + received[...]
    out[...] = value
    top = jnp.max(jnp.abs(value), axis=(0, 1), keepdims=True)
    power = jnp.round(jnp.log2(jnp.maximum(top, 1e-30)))
    rows = value.shape[0]
    scaled[0:rows] = value * jnp.exp2(8.0 - power)
    scaled[rows:] = jnp.broadcast_to(power, (16, value.shape[1]))


def filter_kernel(swap, value, modes, bg_high, bg_low, out):
    which = lax.rem(lax.axis_index("tile") + swap, 2)
    out[...] = value[...] - dot3((bg_high[which], bg_low[which]), split(modes[...]))


def shift(axis, by):
    count = lax.axis_size(axis)
    return [(i, (i + by) % count) for i in range(count)]


def halo(block):
    high = lax.ppermute(block, "tile", shift("tile", -1))
    low = lax.ppermute(block, "tile", shift("tile", 1))
    return low, high


def swap(block):
    return lax.ppermute(block, "tile", [(i, i ^ 1) for i in range(lax.axis_size("tile"))])


def unpacked(sent):
    rows = sent.shape[0] - 16
    return sent[:rows].astype(F32) * jnp.exp2(sent[rows : rows + 1].astype(F32) - 8.0)


def tile_sum(keep, send):
    count = lax.axis_size("tile")
    received = swap(send)
    if count <= 8:
        rows, levels = keep.shape
        block, scaled = call(pack_kernel, (shape(keep.shape, F32), shape((rows + 16, levels), F32)), (keep, received))
        sent = scaled.astype(jnp.float16)
        parts = [lax.ppermute(sent, "tile", [(i, i ^ m) for i in range(count)]) for m in reversed(range(2, count, 2))]
        return sum((unpacked(part) for part in parts), block)
    block = keep + received
    for m in [1 << k for k in range(1, count.bit_length() - 1)]:
        block = block + lax.ppermute(block, "tile", [(i, i ^ m) for i in range(count)])
    return block


def body(fields, velocity, operators, neighbours, kappa_ref, quad_weight, basis, degree):
    nodes, nfield, levels = fields.shape
    blocks, _, size, _ = operators.shape
    modes = basis.shape[1]
    rads = lax.axis_size("rad")
    fields = fields.reshape(nodes, levels)
    velocity = velocity.reshape(2 * nodes, levels)
    wide = shape((nodes, levels), F32)
    thin = shape((nodes, levels), BF)

    dhat = cheb_matrix(rads * levels)
    dhat = np.stack([dhat[:, c * levels : (c + 1) * levels] for c in range(rads)])
    dh_high = dhat.astype(BF)
    dh_low = (dhat - dh_high.astype(np.float32)).astype(BF)

    half = shape((modes // 2, levels), F32)
    dma = pltpu.SemaphoreType.DMA
    fields, rounded, ids = call(
        round_kernel,
        (wide, thin, shape(neighbours.shape, neighbours.dtype)),
        (fields, neighbours),
        "hh",
        (dma((3,)), dma(())),
    )
    low, high = halo(rounded)
    lap_dense, lap_own = call(
        prepare_kernel,
        (shape((3 * blocks, nodes, size), BF), wide),
        (ids, operators, rounded),
        "shv",
        (pltpu.VMEM((blocks, size, operators.shape[3]), BF), dma((blocks,))),
    )
    lap = call(first_lap_kernel, thin, (lap_dense, lap_own, high, low))
    low_two, high_two = halo(lap)
    part = call(
        advect_kernel,
        wide,
        (ids, operators, velocity, lap_dense, low, rounded, high, lap, fields),
        "svvvvvvvv",
        (pltpu.VMEM((3 * nodes, levels), BF),),
    )
    stepped, narrow = call(second_lap_kernel, (wide, thin), (lap_dense, high_two, low_two, part))
    order = [0, *reversed(range(1, rads))]
    shards = [narrow] + [lax.ppermute(narrow, "rad", [(source(i, d), i) for i in range(rads)]) for d in order[1:]]
    wbt, early, bg_high, bg_low = call(
        project_kernel,
        (shape((modes, nodes), BF), shape((modes, levels), F32)) + (shape((2, nodes, modes // 2), BF),) * 2,
        (basis, quad_weight[None, :], degree[None, :], stepped),
        "hhhv",
        (pltpu.VMEM((nodes, modes), F32), pltpu.VMEM((1, nodes), F32), pltpu.VMEM((1, modes), jnp.int32), dma((3,))),
    )
    dhat = (jnp.asarray(dh_high), jnp.asarray(dh_low), kappa_ref.reshape(rads, 1, levels))
    slopes, rates = call(
        lambda *refs: early_diffuse_kernel(order, *refs),
        (shape((nodes, rads * levels), F32), shape((nodes, (rads - 1) * levels), F32)),
        (*shards[:-1], *dhat),
    )
    diffused, keep, send = call(
        lambda *refs: diffuse_kernel(order, *refs),
        (wide, half, half),
        (shards[-1], stepped, *dhat, wbt, early, slopes, rates),
    )
    mine = tile_sum(keep, send)
    other = swap(mine)
    some = call(lambda *refs: filter_kernel(0, *refs), wide, (diffused, mine, bg_high, bg_low))
    filtered = call(lambda *refs: filter_kernel(1, *refs), wide, (some, other, bg_high, bg_low))
    return filtered.reshape(nodes, nfield, levels)


def solution(mesh):
    return jax.shard_map(
        body,
        mesh=mesh,
        in_specs=(
            P("tile", None, "rad"),
            P("tile", None, "rad"),
            P("tile", None, None, None),
            P("tile", None),
            P(),
            P("tile"),
            P("tile", None),
            P(),
        ),
        out_specs=P("tile", None, "rad"),
        check_vma=False,
    )
```

```python
import math

import jax
import jax.numpy as jnp
import numpy as np
from jax import lax
from jax.experimental import pallas as pl
from jax.experimental.pallas import tpu as pltpu
from jax.sharding import PartitionSpec as P

DEGMAX = 22

advect_step = 0.25
hyper_rate = 0.1
radial_step = 0.25

BF = jnp.bfloat16
F32 = jnp.float32
VMEM = pl.BlockSpec(memory_space=pltpu.VMEM)
SMEM = pl.BlockSpec(memory_space=pltpu.SMEM)
HBM = pl.BlockSpec(memory_space=pltpu.HBM)
PARAMS = pltpu.CompilerParams(vmem_limit_bytes=32 * 1024 * 1024)


def cheb_matrix(count):
    points = np.arange(count)
    angles = np.pi * points / (count - 1)
    upper, lower = angles[:, None], angles[None, :]
    spacing = -2.0 * np.sin((upper + lower) / 2.0) * np.sin((upper - lower) / 2.0)
    np.fill_diagonal(spacing, 1.0)
    weights = np.where((points == 0) | (points == count - 1), 2.0, 1.0)
    parity = np.where((upper * 0 + points[:, None] + points[None, :]) % 2 == 0, 1.0, -1.0)
    entries = weights[:, None] / weights[None, :] * parity / spacing
    np.fill_diagonal(entries, 0.0)
    matrix = entries - np.diag(entries.sum(axis=1))
    return (np.sin(angles)[:, None] * matrix / count).T.astype(np.float32)


def split(value):
    high = value.astype(BF)
    return high, (value - high.astype(F32)).astype(BF)


def dot(left, right):
    return jnp.dot(left, right, preferred_element_type=F32)


def dot3(left, right):
    wide = dot(left[0], jnp.concatenate(right, axis=1))
    count = right[0].shape[1]
    return wide[:, :count] + (wide[:, count:] + dot(left[1], right[0]))


def call(kernel, outs, args, spaces=None, scratch=()):
    spaces = spaces or "v" * len(args)
    args = [pltpu.with_memory_space_constraint(a, pltpu.HBM) if c == "h" else a for a, c in zip(args, spaces)]
    return pl.pallas_call(
        kernel,
        out_shape=outs,
        in_specs=[{"s": SMEM, "h": HBM, "v": VMEM}[c] for c in spaces],
        out_specs=jax.tree.map(lambda _: VMEM, outs),
        scratch_shapes=list(scratch),
        compiler_params=PARAMS,
    )(*args)


def shape(dims, kind):
    return jax.ShapeDtypeStruct(dims, kind)


def beside(dense, first, count):
    return jnp.concatenate([dense[first + s] for s in range(count)], axis=1)


def local_id(ids, b, k, blocks):
    total = blocks * lax.axis_size("tile")
    return lax.rem(ids[b, k] - (lax.axis_index("tile") - 1) * blocks + total, total)


def round_kernel(fields, neighbours, wide, narrow, ids, sems, ids_sem):
    parts = sems.shape[0]
    rows = wide.shape[0] // parts
    copies = []
    for p in range(parts):
        piece = pl.ds(p * rows, rows)
        copies.append(pltpu.make_async_copy(fields.at[piece], wide.at[piece], sems.at[p]))
        copies[-1].start()
    ids_copy = pltpu.make_async_copy(neighbours, ids, ids_sem)
    ids_copy.start()
    for p in range(parts):
        copies[p].wait()
        piece = slice(p * rows, (p + 1) * rows)
        narrow[piece] = wide[piece].astype(BF)
    ids_copy.wait()


def prepare_kernel(ids, ops, own, dense, lap_own, held, sems):
    blocks, _, size, wide = ops.shape
    copies = [pltpu.make_async_copy(ops.at[b, 2], held.at[b], sems.at[b]) for b in range(blocks)]
    for copy in copies:
        copy.start()
    dense[...] = jnp.zeros(dense.shape, BF)
    for b in range(blocks):
        copies[b].wait()
        for k in range(wide // size):
            dense[local_id(ids, b, k, blocks), b * size : (b + 1) * size, :] = held[b, :, k * size : (k + 1) * size]
    lap_own[...] = dot(beside(dense, blocks, blocks), own[...])


def around(dense, low, high):
    blocks = dense.shape[0] // 3
    return dot(beside(dense, 0, blocks), low[...]) + dot(beside(dense, 2 * blocks, blocks), high[...])


def first_lap_kernel(dense, lap_own, high, low, lap):
    lap[...] = (lap_own[...] + around(dense, low, high)).astype(BF)


def advect_kernel(ids, ops, velocity, lap_dense, low, own, high, lap, fields, out, window):
    blocks, _, size, wide = ops.shape
    nodes = own.shape[0]
    for k, tile in enumerate((low, own, high)):
        window[k * nodes : (k + 1) * nodes] = tile[...]
    lap_two = dot(beside(lap_dense, blocks, blocks), lap[...])
    for b in range(blocks):
        starts = [pl.multiple_of(local_id(ids, b, k, blocks) * size, size) for k in range(wide // size)]
        nearby = jnp.concatenate([window[pl.ds(start, size), :] for start in starts], axis=0)
        grad = dot(ops[b, 0:2].reshape(2 * size, wide), nearby)
        vel_x = velocity[pl.ds(2 * b * size, size, stride=2), :]
        vel_y = velocity[pl.ds(2 * b * size + 1, size, stride=2), :]
        rows = slice(b * size, (b + 1) * size)
        value = fields[rows] - advect_step * (vel_x * grad[:size] + vel_y * grad[size:])
        out[rows] = value - hyper_rate * lap_two[rows]


def second_lap_kernel(dense, high, low, part, stepped, narrow):
    value = part[...] - hyper_rate * around(dense, low, high)
    stepped[...] = value
    narrow[...] = value.astype(BF)


def project_kernel(basis, weight, degree, value, wbt, early, bg_high, bg_low, held, weight_held, degree_held, sems):
    nodes, modes = held.shape
    pairs = ((basis, held), (weight, weight_held), (degree, degree_held))
    copies = [pltpu.make_async_copy(*pair, sems.at[k]) for k, pair in enumerate(pairs)]
    for copy in copies:
        copy.start()
    for copy in copies:
        copy.wait()
    parts = split(held[...].T * weight_held[...])
    wbt[...] = parts[0]
    early[...] = dot3(parts, split(value[...]))
    ratio = degree_held[...].astype(F32) / DEGMAX
    gain = 0.5 * math.sqrt(modes / (nodes * lax.axis_size("tile"))) * (1.0 - jnp.exp(-4.0 * ratio * ratio))
    half = modes // 2
    for c in range(2):
        cols = slice(c * half, (c + 1) * half)
        bg_high[c], bg_low[c] = split(held[:, cols] * gain[:, cols])


def source(rad, d):
    count = lax.axis_size("rad")
    return (rad + count - d) % count if isinstance(rad, int) else lax.rem(rad + count - d, count)


def gathered(order, width):
    rad = lax.axis_index("rad")
    chunk = [source(rad, d) for d in order]
    return rad, chunk, [pl.ds(pl.multiple_of(c * width, width), width) for c in chunk]


def early_diffuse_kernel(order, *refs):
    count = len(order)
    shards = refs[: count - 1]
    dh_high, dh_low, kappa, slopes, rates = refs[count - 1 :]
    width = kappa.shape[2]
    _, chunk, rows = gathered(order, width)
    value = jnp.concatenate([shard[...] for shard in shards], axis=1)
    total = None
    for table in (dh_high, dh_low):
        weights = [jnp.concatenate([table[c, r, :] for r in rows[:-1]], axis=0) for c in chunk]
        more = dot(value, jnp.concatenate(weights, axis=1))
        total = more if total is None else total + more
    slopes[...] = total
    rate = jnp.concatenate([kappa[c] for c in chunk[:-1]], axis=1)
    rates[...] = rate + (0.5 * rate) * jnp.tanh(value.astype(F32))


def diffuse_kernel(order, last, dh_high, dh_low, kappa, wbt, early, slopes, rates, late, send):
    width = last.shape[1]
    rad, chunk, rows = gathered(order, width)
    core = lax.rem(lax.axis_index("tile"), 2)
    value = last[...]
    weights = [jnp.concatenate([dh_high[c, rows[-1], :], dh_low[c, rows[-1], :]], axis=0) for c in chunk]
    total = slopes[...] + dot(jnp.concatenate([value, value], axis=1), jnp.concatenate(weights, axis=1))
    rate = kappa[chunk[-1]]
    last_rates = rate + (0.5 * rate) * jnp.tanh(value.astype(F32))
    fluxes = jnp.concatenate([rates[...], last_rates], axis=1) * total
    own = [jnp.concatenate([table[rad, r, :] for r in rows], axis=0) for table in (dh_high, dh_low)]
    late[...] = jnp.concatenate(split(radial_step * dot3(split(fluxes), own)), axis=1)
    send[...] = mode_half(wbt, early, late, 1 - core)


def mode_half(wbt, early, late, which):
    half, width = early.shape[0] // 2, early.shape[1]
    modes = pl.ds(pl.multiple_of(which * half, half), half)
    total = dot(wbt[modes, :], late[...])
    return early[modes, :] + total[:, :width] + total[:, width:]


def keep_kernel(wbt, early, late, stepped, keep, diffused):
    width = stepped.shape[1]
    keep[...] = mode_half(wbt, early, late, lax.rem(lax.axis_index("tile"), 2))
    diffused[...] = stepped[...] + late[:, :width].astype(F32) + late[:, width:].astype(F32)


def pack_kernel(keep, received, out, scaled):
    value = keep[...] + received[...]
    out[...] = value
    top = jnp.max(jnp.abs(value), axis=(0, 1), keepdims=True)
    power = jnp.round(jnp.log2(jnp.maximum(top, 1e-30)))
    rows = value.shape[0]
    scaled[0:rows] = value * jnp.exp2(8.0 - power)
    scaled[rows:] = jnp.broadcast_to(power, (16, value.shape[1]))


def filter_kernel(swap, value, modes, bg_high, bg_low, out):
    which = lax.rem(lax.axis_index("tile") + swap, 2)
    out[...] = value[...] - dot3((bg_high[which], bg_low[which]), split(modes[...]))


def shift(axis, by):
    count = lax.axis_size(axis)
    return [(i, (i + by) % count) for i in range(count)]


def halo(block):
    high = lax.ppermute(block, "tile", shift("tile", -1))
    low = lax.ppermute(block, "tile", shift("tile", 1))
    return low, high


def swap(block):
    return lax.ppermute(block, "tile", [(i, i ^ 1) for i in range(lax.axis_size("tile"))])


def unpacked(sent):
    rows = sent.shape[0] - 16
    return sent[:rows].astype(F32) * jnp.exp2(sent[rows : rows + 1].astype(F32) - 8.0)


def tile_sum(keep, send):
    count = lax.axis_size("tile")
    received = swap(send)
    if count <= 8:
        rows, levels = keep.shape
        block, scaled = call(pack_kernel, (shape(keep.shape, F32), shape((rows + 16, levels), F32)), (keep, received))
        sent = scaled.astype(jnp.float16)
        parts = [lax.ppermute(sent, "tile", [(i, i ^ m) for i in range(count)]) for m in range(2, count, 2)]
        return sum((unpacked(part) for part in parts), block)
    block = keep + received
    for m in [1 << k for k in range(1, count.bit_length() - 1)]:
        block = block + lax.ppermute(block, "tile", [(i, i ^ m) for i in range(count)])
    return block


def body(fields, velocity, operators, neighbours, kappa_ref, quad_weight, basis, degree):
    nodes, nfield, levels = fields.shape
    blocks, _, size, _ = operators.shape
    modes = basis.shape[1]
    rads = lax.axis_size("rad")
    fields = fields.reshape(nodes, levels)
    velocity = velocity.reshape(2 * nodes, levels)
    wide = shape((nodes, levels), F32)
    thin = shape((nodes, levels), BF)

    dhat = cheb_matrix(rads * levels)
    dhat = np.stack([dhat[:, c * levels : (c + 1) * levels] for c in range(rads)])
    dh_high = dhat.astype(BF)
    dh_low = (dhat - dh_high.astype(np.float32)).astype(BF)

    half = shape((modes // 2, levels), F32)
    dma = pltpu.SemaphoreType.DMA
    fields, rounded, ids = call(
        round_kernel,
        (wide, thin, shape(neighbours.shape, neighbours.dtype)),
        (fields, neighbours),
        "hh",
        (dma((3,)), dma(())),
    )
    low, high = halo(rounded)
    lap_dense, lap_own = call(
        prepare_kernel,
        (shape((3 * blocks, nodes, size), BF), wide),
        (ids, operators, rounded),
        "shv",
        (pltpu.VMEM((blocks, size, operators.shape[3]), BF), dma((blocks,))),
    )
    lap = call(first_lap_kernel, thin, (lap_dense, lap_own, high, low))
    low_two, high_two = halo(lap)
    part = call(
        advect_kernel,
        wide,
        (ids, operators, velocity, lap_dense, low, rounded, high, lap, fields),
        "svvvvvvvv",
        (pltpu.VMEM((3 * nodes, levels), BF),),
    )
    stepped, narrow = call(second_lap_kernel, (wide, thin), (lap_dense, high_two, low_two, part))
    order = [0, *reversed(range(1, rads))]
    shards = [narrow] + [lax.ppermute(narrow, "rad", [(source(i, d), i) for i in range(rads)]) for d in order[1:]]
    wbt, early, bg_high, bg_low = call(
        project_kernel,
        (shape((modes, nodes), BF), shape((modes, levels), F32)) + (shape((2, nodes, modes // 2), BF),) * 2,
        (basis, quad_weight[None, :], degree[None, :], stepped),
        "hhhv",
        (pltpu.VMEM((nodes, modes), F32), pltpu.VMEM((1, nodes), F32), pltpu.VMEM((1, modes), jnp.int32), dma((3,))),
    )
    dhat = (jnp.asarray(dh_high), jnp.asarray(dh_low), kappa_ref.reshape(rads, 1, levels))
    slopes, rates = call(
        lambda *refs: early_diffuse_kernel(order, *refs),
        (shape((nodes, rads * levels), F32), shape((nodes, (rads - 1) * levels), F32)),
        (*shards[:-1], *dhat),
    )
    late, send = call(
        lambda *refs: diffuse_kernel(order, *refs),
        (shape((nodes, 2 * levels), BF), half),
        (shards[-1], *dhat, wbt, early, slopes, rates),
    )
    keep, diffused = call(keep_kernel, (half, wide), (wbt, early, late, stepped))
    mine = tile_sum(keep, send)
    other = swap(mine)
    some = call(lambda *refs: filter_kernel(0, *refs), wide, (diffused, mine, bg_high, bg_low))
    filtered = call(lambda *refs: filter_kernel(1, *refs), wide, (some, other, bg_high, bg_low))
    return filtered.reshape(nodes, nfield, levels)


def solution(mesh):
    return jax.shard_map(
        body,
        mesh=mesh,
        in_specs=(
            P("tile", None, "rad"),
            P("tile", None, "rad"),
            P("tile", None, None, None),
            P("tile", None),
            P(),
            P("tile"),
            P("tile", None),
            P(),
        ),
        out_specs=P("tile", None, "rad"),
        check_vma=False,
    )
```

```python
import math

import jax
import jax.numpy as jnp
import numpy as np
from jax import lax
from jax.experimental import pallas as pl
from jax.experimental.pallas import tpu as pltpu
from jax.sharding import PartitionSpec as P

DEGMAX = 22

advect_step = 0.25
hyper_rate = 0.1
radial_step = 0.25

BF = jnp.bfloat16
F32 = jnp.float32
VMEM = pl.BlockSpec(memory_space=pltpu.VMEM)
SMEM = pl.BlockSpec(memory_space=pltpu.SMEM)
HBM = pl.BlockSpec(memory_space=pltpu.HBM)
PARAMS = pltpu.CompilerParams(vmem_limit_bytes=32 * 1024 * 1024)


def cheb_matrix(count):
    points = np.arange(count)
    angles = np.pi * points / (count - 1)
    upper, lower = angles[:, None], angles[None, :]
    spacing = -2.0 * np.sin((upper + lower) / 2.0) * np.sin((upper - lower) / 2.0)
    np.fill_diagonal(spacing, 1.0)
    weights = np.where((points == 0) | (points == count - 1), 2.0, 1.0)
    parity = np.where((upper * 0 + points[:, None] + points[None, :]) % 2 == 0, 1.0, -1.0)
    entries = weights[:, None] / weights[None, :] * parity / spacing
    np.fill_diagonal(entries, 0.0)
    matrix = entries - np.diag(entries.sum(axis=1))
    return (np.sin(angles)[:, None] * matrix / count).T.astype(np.float32)


def split(value):
    high = value.astype(BF)
    return high, (value - high.astype(F32)).astype(BF)


def dot(left, right):
    return jnp.dot(left, right, preferred_element_type=F32)


def dot3(left, right):
    wide = dot(left[0], jnp.concatenate(right, axis=1))
    count = right[0].shape[1]
    return wide[:, :count] + (wide[:, count:] + dot(left[1], right[0]))


def call(kernel, outs, args, spaces=None, scratch=()):
    spaces = spaces or "v" * len(args)
    args = [pltpu.with_memory_space_constraint(a, pltpu.HBM) if c == "h" else a for a, c in zip(args, spaces)]
    return pl.pallas_call(
        kernel,
        out_shape=outs,
        in_specs=[{"s": SMEM, "h": HBM, "v": VMEM}[c] for c in spaces],
        out_specs=jax.tree.map(lambda _: VMEM, outs),
        scratch_shapes=list(scratch),
        compiler_params=PARAMS,
    )(*args)


def shape(dims, kind):
    return jax.ShapeDtypeStruct(dims, kind)


def beside(dense, first, count):
    return jnp.concatenate([dense[first + s] for s in range(count)], axis=1)


def local_id(ids, b, k, blocks):
    total = blocks * lax.axis_size("tile")
    return lax.rem(ids[b, k] - (lax.axis_index("tile") - 1) * blocks + total, total)


def round_kernel(fields, neighbours, wide, narrow, ids, sems, ids_sem):
    parts = sems.shape[0]
    rows = wide.shape[0] // parts
    copies = []
    for p in range(parts):
        piece = pl.ds(p * rows, rows)
        copies.append(pltpu.make_async_copy(fields.at[piece], wide.at[piece], sems.at[p]))
        copies[-1].start()
    ids_copy = pltpu.make_async_copy(neighbours, ids, ids_sem)
    ids_copy.start()
    for p in range(parts):
        copies[p].wait()
        piece = slice(p * rows, (p + 1) * rows)
        narrow[piece] = wide[piece].astype(BF)
    ids_copy.wait()


def prepare_kernel(ids, ops, own, dense, lap_own, held, sems):
    blocks, _, size, wide = ops.shape
    copies = [pltpu.make_async_copy(ops.at[b, 2], held.at[b], sems.at[b]) for b in range(blocks)]
    for copy in copies:
        copy.start()
    dense[...] = jnp.zeros(dense.shape, BF)
    for b in range(blocks):
        copies[b].wait()
        for k in range(wide // size):
            dense[local_id(ids, b, k, blocks), b * size : (b + 1) * size, :] = held[b, :, k * size : (k + 1) * size]
    lap_own[...] = dot(beside(dense, blocks, blocks), own[...])


def around(dense, low, high):
    blocks = dense.shape[0] // 3
    weights = jnp.concatenate([beside(dense, 0, blocks), beside(dense, 2 * blocks, blocks)], axis=1)
    return dot(weights, jnp.concatenate([low[...], high[...]], axis=0))


def first_lap_kernel(dense, lap_own, high, low, lap):
    lap[...] = (lap_own[...] + around(dense, low, high)).astype(BF)


def advect_kernel(ids, ops, velocity, lap_dense, low, own, high, lap, fields, out, window):
    blocks, _, size, wide = ops.shape
    nodes = own.shape[0]
    for k, tile in enumerate((low, own, high)):
        window[k * nodes : (k + 1) * nodes] = tile[...]
    lap_two = dot(beside(lap_dense, blocks, blocks), lap[...])
    for b in range(blocks):
        starts = [pl.multiple_of(local_id(ids, b, k, blocks) * size, size) for k in range(wide // size)]
        nearby = jnp.concatenate([window[pl.ds(start, size), :] for start in starts], axis=0)
        grad = dot(ops[b, 0:2].reshape(2 * size, wide), nearby)
        vel_x = velocity[pl.ds(2 * b * size, size, stride=2), :]
        vel_y = velocity[pl.ds(2 * b * size + 1, size, stride=2), :]
        rows = slice(b * size, (b + 1) * size)
        value = fields[rows] - advect_step * (vel_x * grad[:size] + vel_y * grad[size:])
        out[rows] = value - hyper_rate * lap_two[rows]


def second_lap_kernel(dense, high, low, part, stepped, narrow):
    value = part[...] - hyper_rate * around(dense, low, high)
    stepped[...] = value
    narrow[...] = value.astype(BF)


def project_kernel(basis, weight, degree, value, wbt, early, bg_high, bg_low, held, weight_held, degree_held, sems):
    nodes, modes = held.shape
    pairs = ((basis, held), (weight, weight_held), (degree, degree_held))
    copies = [pltpu.make_async_copy(*pair, sems.at[k]) for k, pair in enumerate(pairs)]
    for copy in copies:
        copy.start()
    for copy in copies:
        copy.wait()
    parts = split(held[...].T * weight_held[...])
    wbt[...] = parts[0]
    early[...] = dot3(parts, split(value[...]))
    ratio = degree_held[...].astype(F32) / DEGMAX
    gain = 0.5 * math.sqrt(modes / (nodes * lax.axis_size("tile"))) * (1.0 - jnp.exp(-4.0 * ratio * ratio))
    half = modes // 2
    for c in range(2):
        cols = slice(c * half, (c + 1) * half)
        bg_high[c], bg_low[c] = split(held[:, cols] * gain[:, cols])


def source(rad, d):
    count = lax.axis_size("rad")
    return (rad + count - d) % count if isinstance(rad, int) else lax.rem(rad + count - d, count)


def gathered(order, width):
    rad = lax.axis_index("rad")
    chunk = [source(rad, d) for d in order]
    return rad, chunk, [pl.ds(pl.multiple_of(c * width, width), width) for c in chunk]


def early_diffuse_kernel(order, *refs):
    count = len(order)
    shards = refs[: count - 1]
    dh_high, dh_low, kappa, slopes, rates = refs[count - 1 :]
    width = kappa.shape[2]
    _, chunk, rows = gathered(order, width)
    value = jnp.concatenate([shard[...] for shard in shards], axis=1)
    total = None
    for table in (dh_high, dh_low):
        weights = [jnp.concatenate([table[c, r, :] for r in rows[:-1]], axis=0) for c in chunk]
        more = dot(value, jnp.concatenate(weights, axis=1))
        total = more if total is None else total + more
    slopes[...] = total
    rate = jnp.concatenate([kappa[c] for c in chunk[:-1]], axis=1)
    rates[...] = rate + (0.5 * rate) * jnp.tanh(value.astype(F32))


def diffuse_kernel(order, last, dh_high, dh_low, kappa, wbt, early, slopes, rates, late, send):
    width = last.shape[1]
    rad, chunk, rows = gathered(order, width)
    core = lax.rem(lax.axis_index("tile"), 2)
    value = last[...]
    weights = [jnp.concatenate([dh_high[c, rows[-1], :], dh_low[c, rows[-1], :]], axis=0) for c in chunk]
    total = slopes[...] + dot(jnp.concatenate([value, value], axis=1), jnp.concatenate(weights, axis=1))
    rate = kappa[chunk[-1]]
    last_rates = rate + (0.5 * rate) * jnp.tanh(value.astype(F32))
    fluxes = jnp.concatenate([rates[...], last_rates], axis=1) * total
    own = [jnp.concatenate([table[rad, r, :] for r in rows], axis=0) for table in (dh_high, dh_low)]
    late[...] = jnp.concatenate(split(radial_step * dot3(split(fluxes), own)), axis=1)
    send[...] = mode_half(wbt, early, late, 1 - core)


def mode_half(wbt, early, late, which):
    half, width = early.shape[0] // 2, early.shape[1]
    modes = pl.ds(pl.multiple_of(which * half, half), half)
    total = dot(wbt[modes, :], late[...])
    return early[modes, :] + total[:, :width] + total[:, width:]


def keep_kernel(wbt, early, late, stepped, keep, diffused):
    width = stepped.shape[1]
    keep[...] = mode_half(wbt, early, late, lax.rem(lax.axis_index("tile"), 2))
    diffused[...] = stepped[...] + late[:, :width].astype(F32) + late[:, width:].astype(F32)


def pack_kernel(keep, received, out, scaled):
    value = keep[...] + received[...]
    out[...] = value
    top = jnp.max(jnp.abs(value), axis=(0, 1), keepdims=True)
    power = jnp.round(jnp.log2(jnp.maximum(top, 1e-30)))
    rows = value.shape[0]
    scaled[0:rows] = value * jnp.exp2(8.0 - power)
    scaled[rows:] = jnp.broadcast_to(power, (16, value.shape[1]))


def filter_kernel(swap, value, modes, bg_high, bg_low, out):
    which = lax.rem(lax.axis_index("tile") + swap, 2)
    out[...] = value[...] - dot3((bg_high[which], bg_low[which]), split(modes[...]))


def shift(axis, by):
    count = lax.axis_size(axis)
    return [(i, (i + by) % count) for i in range(count)]


def halo(block):
    high = lax.ppermute(block, "tile", shift("tile", -1))
    low = lax.ppermute(block, "tile", shift("tile", 1))
    return low, high


def swap(block):
    return lax.ppermute(block, "tile", [(i, i ^ 1) for i in range(lax.axis_size("tile"))])


def unpacked(sent):
    rows = sent.shape[0] - 16
    return sent[:rows].astype(F32) * jnp.exp2(sent[rows : rows + 1].astype(F32) - 8.0)


def tile_sum(keep, send):
    count = lax.axis_size("tile")
    received = swap(send)
    if count <= 8:
        rows, levels = keep.shape
        block, scaled = call(pack_kernel, (shape(keep.shape, F32), shape((rows + 16, levels), F32)), (keep, received))
        sent = scaled.astype(jnp.float16)
        parts = [lax.ppermute(sent, "tile", [(i, i ^ m) for i in range(count)]) for m in range(2, count, 2)]
        return sum((unpacked(part) for part in parts), block)
    block = keep + received
    for m in [1 << k for k in range(1, count.bit_length() - 1)]:
        block = block + lax.ppermute(block, "tile", [(i, i ^ m) for i in range(count)])
    return block


def body(fields, velocity, operators, neighbours, kappa_ref, quad_weight, basis, degree):
    nodes, nfield, levels = fields.shape
    blocks, _, size, _ = operators.shape
    modes = basis.shape[1]
    rads = lax.axis_size("rad")
    fields = fields.reshape(nodes, levels)
    velocity = velocity.reshape(2 * nodes, levels)
    wide = shape((nodes, levels), F32)
    thin = shape((nodes, levels), BF)

    dhat = cheb_matrix(rads * levels)
    dhat = np.stack([dhat[:, c * levels : (c + 1) * levels] for c in range(rads)])
    dh_high = dhat.astype(BF)
    dh_low = (dhat - dh_high.astype(np.float32)).astype(BF)

    half = shape((modes // 2, levels), F32)
    dma = pltpu.SemaphoreType.DMA
    fields, rounded, ids = call(
        round_kernel,
        (wide, thin, shape(neighbours.shape, neighbours.dtype)),
        (fields, neighbours),
        "hh",
        (dma((3,)), dma(())),
    )
    low, high = halo(rounded)
    lap_dense, lap_own = call(
        prepare_kernel,
        (shape((3 * blocks, nodes, size), BF), wide),
        (ids, operators, rounded),
        "shv",
        (pltpu.VMEM((blocks, size, operators.shape[3]), BF), dma((blocks,))),
    )
    lap = call(first_lap_kernel, thin, (lap_dense, lap_own, high, low))
    low_two, high_two = halo(lap)
    part = call(
        advect_kernel,
        wide,
        (ids, operators, velocity, lap_dense, low, rounded, high, lap, fields),
        "svvvvvvvv",
        (pltpu.VMEM((3 * nodes, levels), BF),),
    )
    stepped, narrow = call(second_lap_kernel, (wide, thin), (lap_dense, high_two, low_two, part))
    order = [0, *reversed(range(1, rads))]
    shards = [narrow] + [lax.ppermute(narrow, "rad", [(source(i, d), i) for i in range(rads)]) for d in order[1:]]
    wbt, early, bg_high, bg_low = call(
        project_kernel,
        (shape((modes, nodes), BF), shape((modes, levels), F32)) + (shape((2, nodes, modes // 2), BF),) * 2,
        (basis, quad_weight[None, :], degree[None, :], stepped),
        "hhhv",
        (pltpu.VMEM((nodes, modes), F32), pltpu.VMEM((1, nodes), F32), pltpu.VMEM((1, modes), jnp.int32), dma((3,))),
    )
    dhat = (jnp.asarray(dh_high), jnp.asarray(dh_low), kappa_ref.reshape(rads, 1, levels))
    slopes, rates = call(
        lambda *refs: early_diffuse_kernel(order, *refs),
        (shape((nodes, rads * levels), F32), shape((nodes, (rads - 1) * levels), F32)),
        (*shards[:-1], *dhat),
    )
    late, send = call(
        lambda *refs: diffuse_kernel(order, *refs),
        (shape((nodes, 2 * levels), BF), half),
        (shards[-1], *dhat, wbt, early, slopes, rates),
    )
    keep, diffused = call(keep_kernel, (half, wide), (wbt, early, late, stepped))
    mine = tile_sum(keep, send)
    other = swap(mine)
    some = call(lambda *refs: filter_kernel(0, *refs), wide, (diffused, mine, bg_high, bg_low))
    filtered = call(lambda *refs: filter_kernel(1, *refs), wide, (some, other, bg_high, bg_low))
    return filtered.reshape(nodes, nfield, levels)


def solution(mesh):
    return jax.shard_map(
        body,
        mesh=mesh,
        in_specs=(
            P("tile", None, "rad"),
            P("tile", None, "rad"),
            P("tile", None, None, None),
            P("tile", None),
            P(),
            P("tile"),
            P("tile", None),
            P(),
        ),
        out_specs=P("tile", None, "rad"),
        check_vma=False,
    )
```

```python
import math

import jax
import jax.numpy as jnp
import numpy as np
from jax import lax
from jax.experimental import pallas as pl
from jax.experimental.pallas import tpu as pltpu
from jax.sharding import PartitionSpec as P

DEGMAX = 22

advect_step = 0.25
hyper_rate = 0.1
radial_step = 0.25

BF = jnp.bfloat16
F32 = jnp.float32
VMEM = pl.BlockSpec(memory_space=pltpu.VMEM)
SMEM = pl.BlockSpec(memory_space=pltpu.SMEM)
HBM = pl.BlockSpec(memory_space=pltpu.HBM)
PARAMS = pltpu.CompilerParams(vmem_limit_bytes=32 * 1024 * 1024)


def cheb_matrix(count):
    points = np.arange(count)
    angles = np.pi * points / (count - 1)
    upper, lower = angles[:, None], angles[None, :]
    spacing = -2.0 * np.sin((upper + lower) / 2.0) * np.sin((upper - lower) / 2.0)
    np.fill_diagonal(spacing, 1.0)
    weights = np.where((points == 0) | (points == count - 1), 2.0, 1.0)
    parity = np.where((upper * 0 + points[:, None] + points[None, :]) % 2 == 0, 1.0, -1.0)
    entries = weights[:, None] / weights[None, :] * parity / spacing
    np.fill_diagonal(entries, 0.0)
    matrix = entries - np.diag(entries.sum(axis=1))
    return (np.sin(angles)[:, None] * matrix / count).T.astype(np.float32)


def split(value):
    high = value.astype(BF)
    return high, (value - high.astype(F32)).astype(BF)


def dot(left, right):
    return jnp.dot(left, right, preferred_element_type=F32)


def dot3(left, right):
    wide = dot(left[0], jnp.concatenate(right, axis=1))
    count = right[0].shape[1]
    return wide[:, :count] + (wide[:, count:] + dot(left[1], right[0]))


def call(kernel, outs, args, spaces=None, scratch=()):
    spaces = spaces or "v" * len(args)
    args = [pltpu.with_memory_space_constraint(a, pltpu.HBM) if c == "h" else a for a, c in zip(args, spaces)]
    return pl.pallas_call(
        kernel,
        out_shape=outs,
        in_specs=[{"s": SMEM, "h": HBM, "v": VMEM}[c] for c in spaces],
        out_specs=jax.tree.map(lambda _: VMEM, outs),
        scratch_shapes=list(scratch),
        compiler_params=PARAMS,
    )(*args)


def shape(dims, kind):
    return jax.ShapeDtypeStruct(dims, kind)


def beside(dense, first, count):
    return jnp.concatenate([dense[first + s] for s in range(count)], axis=1)


def local_id(ids, b, k, blocks):
    total = blocks * lax.axis_size("tile")
    return lax.rem(ids[b, k] - (lax.axis_index("tile") - 1) * blocks + total, total)


def round_kernel(fields, neighbours, wide, narrow, ids, sems, ids_sem):
    parts = sems.shape[0]
    rows = wide.shape[0] // parts
    copies = []
    for p in range(parts):
        piece = pl.ds(p * rows, rows)
        copies.append(pltpu.make_async_copy(fields.at[piece], wide.at[piece], sems.at[p]))
        copies[-1].start()
    ids_copy = pltpu.make_async_copy(neighbours, ids, ids_sem)
    ids_copy.start()
    for p in range(parts):
        copies[p].wait()
        piece = slice(p * rows, (p + 1) * rows)
        narrow[piece] = wide[piece].astype(BF)
    ids_copy.wait()


def prepare_kernel(ids, ops, own, dense, lap_own, held, sems):
    blocks, _, size, wide = ops.shape
    copies = [pltpu.make_async_copy(ops.at[b, 2], held.at[b], sems.at[b]) for b in range(blocks)]
    for copy in copies:
        copy.start()
    dense[...] = jnp.zeros(dense.shape, BF)
    for b in range(blocks):
        copies[b].wait()
        for k in range(wide // size):
            dense[local_id(ids, b, k, blocks), b * size : (b + 1) * size, :] = held[b, :, k * size : (k + 1) * size]
    lap_own[...] = dot(beside(dense, blocks, blocks), own[...])


def around(dense, low, high):
    blocks = dense.shape[0] // 3
    weights = jnp.concatenate([beside(dense, 0, blocks), beside(dense, 2 * blocks, blocks)], axis=1)
    return dot(weights, jnp.concatenate([low[...], high[...]], axis=0))


def first_lap_kernel(dense, lap_own, high, low, lap):
    lap[...] = (lap_own[...] + around(dense, low, high)).astype(BF)


def advect_kernel(ids, ops, velocity, lap_dense, low, own, high, lap, fields, out, window):
    blocks, _, size, wide = ops.shape
    nodes = own.shape[0]
    for k, tile in enumerate((low, own, high)):
        window[k * nodes : (k + 1) * nodes] = tile[...]
    lap_two = dot(beside(lap_dense, blocks, blocks), lap[...])
    for b in range(blocks):
        starts = [pl.multiple_of(local_id(ids, b, k, blocks) * size, size) for k in range(wide // size)]
        nearby = jnp.concatenate([window[pl.ds(start, size), :] for start in starts], axis=0)
        grad = dot(ops[b, 0:2].reshape(2 * size, wide), nearby)
        vel_x = velocity[pl.ds(2 * b * size, size, stride=2), :]
        vel_y = velocity[pl.ds(2 * b * size + 1, size, stride=2), :]
        rows = slice(b * size, (b + 1) * size)
        value = fields[rows] - advect_step * (vel_x * grad[:size] + vel_y * grad[size:])
        out[rows] = value - hyper_rate * lap_two[rows]


def second_lap_kernel(dense, high, low, part, stepped, narrow):
    value = part[...] - hyper_rate * around(dense, low, high)
    stepped[...] = value
    narrow[...] = value.astype(BF)


def project_kernel(basis, weight, degree, value, wbt, early, bg_high, bg_low, held, weight_held, degree_held, sems):
    nodes, modes = held.shape
    pairs = ((basis, held), (weight, weight_held), (degree, degree_held))
    copies = [pltpu.make_async_copy(*pair, sems.at[k]) for k, pair in enumerate(pairs)]
    for copy in copies:
        copy.start()
    for copy in copies:
        copy.wait()
    parts = split(held[...].T * weight_held[...])
    wbt[...] = parts[0]
    early[...] = dot3(parts, split(value[...]))
    ratio = degree_held[...].astype(F32) / DEGMAX
    gain = 0.5 * math.sqrt(modes / (nodes * lax.axis_size("tile"))) * (1.0 - jnp.exp(-4.0 * ratio * ratio))
    half = modes // 2
    for c in range(2):
        cols = slice(c * half, (c + 1) * half)
        bg_high[c], bg_low[c] = split(held[:, cols] * gain[:, cols])


def source(rad, d):
    count = lax.axis_size("rad")
    return (rad + count - d) % count if isinstance(rad, int) else lax.rem(rad + count - d, count)


def gathered(order, width):
    rad = lax.axis_index("rad")
    chunk = [source(rad, d) for d in order]
    return rad, chunk, [pl.ds(pl.multiple_of(c * width, width), width) for c in chunk]


def early_diffuse_kernel(order, *refs):
    count = len(order)
    shards = refs[: count - 1]
    dh_high, dh_low, kappa, slopes, rates = refs[count - 1 :]
    width = kappa.shape[2]
    _, chunk, rows = gathered(order, width)
    value = jnp.concatenate([shard[...] for shard in shards], axis=1)
    pieces = [(table, r) for table in (dh_high, dh_low) for r in rows[:-1]]
    weights = [jnp.concatenate([table[c, r, :] for table, r in pieces], axis=0) for c in chunk]
    slopes[...] = dot(jnp.concatenate([value, value], axis=1), jnp.concatenate(weights, axis=1))
    rate = jnp.concatenate([kappa[c] for c in chunk[:-1]], axis=1)
    rates[...] = rate + (0.5 * rate) * jnp.tanh(value.astype(F32))


def diffuse_kernel(order, last, dh_high, dh_low, kappa, wbt, early, slopes, rates, late, send):
    width = last.shape[1]
    rad, chunk, rows = gathered(order, width)
    core = lax.rem(lax.axis_index("tile"), 2)
    value = last[...]
    weights = [jnp.concatenate([dh_high[c, rows[-1], :], dh_low[c, rows[-1], :]], axis=0) for c in chunk]
    total = slopes[...] + dot(jnp.concatenate([value, value], axis=1), jnp.concatenate(weights, axis=1))
    rate = kappa[chunk[-1]]
    last_rates = rate + (0.5 * rate) * jnp.tanh(value.astype(F32))
    fluxes = jnp.concatenate([rates[...], last_rates], axis=1) * total
    own = [jnp.concatenate([table[rad, r, :] for r in rows], axis=0) for table in (dh_high, dh_low)]
    late[...] = jnp.concatenate(split(radial_step * dot3(split(fluxes), own)), axis=1)
    send[...] = mode_half(wbt, early, late, 1 - core)


def mode_half(wbt, early, late, which):
    half, width = early.shape[0] // 2, early.shape[1]
    modes = pl.ds(pl.multiple_of(which * half, half), half)
    total = dot(wbt[modes, :], late[...])
    return early[modes, :] + total[:, :width] + total[:, width:]


def keep_kernel(wbt, early, late, stepped, keep, diffused):
    width = stepped.shape[1]
    keep[...] = mode_half(wbt, early, late, lax.rem(lax.axis_index("tile"), 2))
    diffused[...] = stepped[...] + late[:, :width].astype(F32) + late[:, width:].astype(F32)


def pack_kernel(keep, received, out, scaled):
    value = keep[...] + received[...]
    out[...] = value
    top = jnp.max(jnp.abs(value), axis=(0, 1), keepdims=True)
    power = jnp.round(jnp.log2(jnp.maximum(top, 1e-30)))
    rows = value.shape[0]
    scaled[0:rows] = value * jnp.exp2(8.0 - power)
    scaled[rows:] = jnp.broadcast_to(power, (16, value.shape[1]))


def filter_kernel(swap, value, modes, bg_high, bg_low, out):
    which = lax.rem(lax.axis_index("tile") + swap, 2)
    out[...] = value[...] - dot3((bg_high[which], bg_low[which]), split(modes[...]))


def shift(axis, by):
    count = lax.axis_size(axis)
    return [(i, (i + by) % count) for i in range(count)]


def halo(block):
    high = lax.ppermute(block, "tile", shift("tile", -1))
    low = lax.ppermute(block, "tile", shift("tile", 1))
    return low, high


def swap(block):
    return lax.ppermute(block, "tile", [(i, i ^ 1) for i in range(lax.axis_size("tile"))])


def unpacked(sent):
    rows = sent.shape[0] - 16
    return sent[:rows].astype(F32) * jnp.exp2(sent[rows : rows + 1].astype(F32) - 8.0)


def tile_sum(keep, send):
    count = lax.axis_size("tile")
    received = swap(send)
    if count <= 8:
        rows, levels = keep.shape
        block, scaled = call(pack_kernel, (shape(keep.shape, F32), shape((rows + 16, levels), F32)), (keep, received))
        sent = scaled.astype(jnp.float16)
        parts = [lax.ppermute(sent, "tile", [(i, i ^ m) for i in range(count)]) for m in range(2, count, 2)]
        return sum((unpacked(part) for part in parts), block)
    block = keep + received
    for m in [1 << k for k in range(1, count.bit_length() - 1)]:
        block = block + lax.ppermute(block, "tile", [(i, i ^ m) for i in range(count)])
    return block


def body(fields, velocity, operators, neighbours, kappa_ref, quad_weight, basis, degree):
    nodes, nfield, levels = fields.shape
    blocks, _, size, _ = operators.shape
    modes = basis.shape[1]
    rads = lax.axis_size("rad")
    fields = fields.reshape(nodes, levels)
    velocity = velocity.reshape(2 * nodes, levels)
    wide = shape((nodes, levels), F32)
    thin = shape((nodes, levels), BF)

    dhat = cheb_matrix(rads * levels)
    dhat = np.stack([dhat[:, c * levels : (c + 1) * levels] for c in range(rads)])
    dh_high = dhat.astype(BF)
    dh_low = (dhat - dh_high.astype(np.float32)).astype(BF)

    half = shape((modes // 2, levels), F32)
    dma = pltpu.SemaphoreType.DMA
    fields, rounded, ids = call(
        round_kernel,
        (wide, thin, shape(neighbours.shape, neighbours.dtype)),
        (fields, neighbours),
        "hh",
        (dma((3,)), dma(())),
    )
    low, high = halo(rounded)
    lap_dense, lap_own = call(
        prepare_kernel,
        (shape((3 * blocks, nodes, size), BF), wide),
        (ids, operators, rounded),
        "shv",
        (pltpu.VMEM((blocks, size, operators.shape[3]), BF), dma((blocks,))),
    )
    lap = call(first_lap_kernel, thin, (lap_dense, lap_own, high, low))
    low_two, high_two = halo(lap)
    part = call(
        advect_kernel,
        wide,
        (ids, operators, velocity, lap_dense, low, rounded, high, lap, fields),
        "svvvvvvvv",
        (pltpu.VMEM((3 * nodes, levels), BF),),
    )
    stepped, narrow = call(second_lap_kernel, (wide, thin), (lap_dense, high_two, low_two, part))
    order = [0, *reversed(range(1, rads))]
    shards = [narrow] + [lax.ppermute(narrow, "rad", [(source(i, d), i) for i in range(rads)]) for d in order[1:]]
    wbt, early, bg_high, bg_low = call(
        project_kernel,
        (shape((modes, nodes), BF), shape((modes, levels), F32)) + (shape((2, nodes, modes // 2), BF),) * 2,
        (basis, quad_weight[None, :], degree[None, :], stepped),
        "hhhv",
        (pltpu.VMEM((nodes, modes), F32), pltpu.VMEM((1, nodes), F32), pltpu.VMEM((1, modes), jnp.int32), dma((3,))),
    )
    dhat = (jnp.asarray(dh_high), jnp.asarray(dh_low), kappa_ref.reshape(rads, 1, levels))
    slopes, rates = call(
        lambda *refs: early_diffuse_kernel(order, *refs),
        (shape((nodes, rads * levels), F32), shape((nodes, (rads - 1) * levels), F32)),
        (*shards[:-1], *dhat),
    )
    late, send = call(
        lambda *refs: diffuse_kernel(order, *refs),
        (shape((nodes, 2 * levels), BF), half),
        (shards[-1], *dhat, wbt, early, slopes, rates),
    )
    keep, diffused = call(keep_kernel, (half, wide), (wbt, early, late, stepped))
    mine = tile_sum(keep, send)
    other = swap(mine)
    some = call(lambda *refs: filter_kernel(0, *refs), wide, (diffused, mine, bg_high, bg_low))
    filtered = call(lambda *refs: filter_kernel(1, *refs), wide, (some, other, bg_high, bg_low))
    return filtered.reshape(nodes, nfield, levels)


def solution(mesh):
    return jax.shard_map(
        body,
        mesh=mesh,
        in_specs=(
            P("tile", None, "rad"),
            P("tile", None, "rad"),
            P("tile", None, None, None),
            P("tile", None),
            P(),
            P("tile"),
            P("tile", None),
            P(),
        ),
        out_specs=P("tile", None, "rad"),
        check_vma=False,
    )
```
